128 devices in a mesh: ctx: 64 (over y, z_hi, x, core), tp: 2 (over z_lo).
Axes of the slice: x: 4, y: 4, z: 4 (z_hi: 2, z_lo: 2; z = z_hi * 2 + z_lo), core: 2. Of those that a mesh axis runs over, the one named last changes fastest.
Arguments:
- residual: bfloat16 [16384, 5120], P('ctx', 'tp'), may hold values from -6 to 6
- shared_out: bfloat16 [16384, 5120], P('ctx', 'tp'), may hold values from -4 to 4
- expert_out: bfloat16 [128, 64, 4, 5120], P('ctx', None, None, 'tp'), may hold values from -6 to 6
- routing: int32 [16384, 1], P('ctx'), may hold values from 0 to 127; in each aligned block of 256 rows (0 to 255, 256 to 511, ...) at most 4 rows name the same one
- gate_score: float32 [16384, 1], P('ctx'), may hold values from 0.1 to 1
- norm_gain: bfloat16 [5120], replicated, may hold values from 0.25 to 1.75
- w_query: bfloat16 [5120, 2560], P(None, 'tp'), may hold values from -2 to 2
- w_key: bfloat16 [5120, 512], P(None, 'tp'), may hold values from -1 to 1
- w_value: bfloat16 [5120, 512], P(None, 'tp'), may hold values from -0.078125 to 0.078125
Outputs:
- hidden_state: bfloat16 [16384, 5120], P('ctx', 'tp')
- attended: bfloat16 [16384, 2560], P('ctx', 'tp')
The draws below stay inside these ranges and needn't reach their ends.
Inputs may be any that keep to these rules, and one draw needn't show every extreme that they name: `routing`: in each device's aligned block of 256 rows no expert is named by more than 4 rows, a bound that some block reaches.
All inputs are finite; a program needn't handle non-finite values.
Results may differ from the reference program's by a relative error of at most 0.014.
Values may be sent and summed in bfloat16 or wider, within the bound.
No kernel may reach another device: no remote copies, remote signals or barrier semaphores. Data moves between devices by JAX's collectives and lax.ppermute only.
A program may use at most 128 MiB of HBM per device.

```python
import math
import jax
import jax.numpy as jnp
import numpy as np
from jax import lax

D = 5120
QH = 20
KVH = 4
HD = 128
TOK_DEV = 256
EXPERTS = 128
CAP = 4
TOKENS = 16384
N_CTX = 64


def key_columns(key):
    shared_cols = jax.random.normal(key, (D, KVH * HD), jnp.float32)
    return jnp.clip(shared_cols, -4.0, 4.0)


def draw_w_key(key, part):
    shared_cols = key_columns(key)
    return (shared_cols * D ** (-0.5)).astype(jnp.bfloat16)


def draw_w_query(key, part):
    key = jax.random.fold_in(key, 11)
    noise_cols = jnp.clip(jax.random.normal(key, (D, QH * HD), jnp.float32), -4.0, 4.0)
    combined = noise_cols
    return jnp.clip(combined * D ** (-0.5), -2.0, 2.0).astype(jnp.bfloat16)


def block_scale(key, dims, pieces, smallest, top_value):
    factor_of = 1.0
    for dim, blocks in pieces:
        heights = jax.random.uniform(jax.random.fold_in(jax.random.fold_in(key, 6), dim), (blocks,), jnp.float32, smallest / len(pieces), top_value / len(pieces))
        factor_of = factor_of * jnp.repeat(jnp.exp(heights), dims[dim] // blocks).reshape((-1,) + (1,) * (len(dims) - 1 - dim))
    return factor_of


def deal_out(key, own, number, rows, amount, top, reach, slope):
    order = jax.random.permutation(key, amount)
    crowded, usual = load_shares(amount, rows * top, reach, slope, True), load_shares(amount, rows * top, reach, slope, False)
    places = jnp.arange(amount)

    def named(tallies, rotation):
        used = int((tallies > 0).sum())
        fixed = max(1, used // 4)
        shifted = fixed + (places - fixed + rotation * (used - fixed)) % max(1, amount - fixed)
        return jnp.zeros((amount,), jnp.int32).at[order[jnp.where(places < fixed, places, shifted)]].set(jnp.asarray(tallies, jnp.int32))

    tallies = jnp.where(number % 4 == 0, named(crowded, number // 4), named(usual, number - number // 4 - 1))
    mixed = jax.random.permutation(jax.random.fold_in(own, 3), amount)
    source_of, sink = mixed[0:amount // 2 * 2:2], mixed[1:amount // 2 * 2:2]
    slack = jnp.minimum(tallies[source_of] - 1, reach - tallies[sink]) // 2
    slack = jnp.where((source_of == order[0]) | (sink == order[0]) | (tallies[sink] == 0), 0, jnp.maximum(slack, 0))
    shifted = jax.random.randint(jax.random.fold_in(own, 4), (amount // 2,), 0, 1 << 20) % (slack + 1)
    tallies = tallies.at[source_of].add(-shifted).at[sink].add(shifted)
    items = jnp.searchsorted(jnp.cumsum(tallies), jnp.arange(rows * top), side="right").astype(jnp.int32)
    table = items.reshape(top, rows).T
    table = table[jax.random.permutation(jax.random.fold_in(own, 1), rows)]
    rotation = jax.random.randint(jax.random.fold_in(own, 2), (rows, 1), 0, top)
    return jnp.take_along_axis(table, (jnp.arange(top)[None, :] + rotation) % top, axis=1)


def load_shares(number_of, total, reach, skew, full):
    portions = [(1 << 20) // math.isqrt(rank ** skew) + 1 for rank in range(1, number_of + 1)]
    largest = reach if full else min(reach, max(-(-total // number_of), total * portions[0] // sum(portions)))
    least = 1 if total - largest >= number_of - 1 else 0
    given, surplus = [largest] + [least] * (number_of - 1), total - largest - least * (number_of - 1)
    while surplus > 0:
        free = [i for i in range(1, number_of) if given[i] < largest] or [i for i in range(1, number_of) if given[i] < reach]
        whole, remaining = sum([portions[i] for i in free]), surplus
        for i in free:
            more = min(reach - given[i], max(1, remaining * portions[i] // whole), surplus)
            given[i] = given[i] + more
            surplus = surplus - more
    return np.array(given)


def noise(rng, extent, scale, most, shards=(), kind=jnp.bfloat16):
    array = jax.random.normal(rng, extent, jnp.float32) * scale
    if len(shards) > 0:
        array = block_scale(rng, extent, shards, -0.22, 0.18) * array
    return jnp.clip(array, min=-most, max=most).astype(kind)


def setup_inputs(seed: int = 0) -> dict:
    seeds = jax.random.split(jax.random.key(seed), 10)
    residual = noise(seeds[0], (TOKENS, D), 1.0, 6.0, ((0, 64), (1, 2)))
    shared_out = noise(seeds[1], (TOKENS, D), 0.5, 4.0, ((0, 64), (1, 2)))
    expert_out = noise(seeds[2], (EXPERTS, N_CTX, CAP, D), 1.0, 6.0, ((0, 64), (3, 2)))
    routing_keys = jax.random.split(jax.random.fold_in(seeds[3], 1), TOKENS // TOK_DEV)
    routing_turns = jax.random.permutation(jax.random.fold_in(seeds[3], 3), TOKENS // TOK_DEV)
    routing = jax.vmap(lambda own, number: deal_out(jax.random.fold_in(seeds[3], 2), own, number, TOK_DEV, EXPERTS, 1, CAP, 2))(routing_keys, routing_turns).reshape((TOKENS, 1))
    gate_score = jnp.clip(0.1 + 0.9 * jax.random.uniform(seeds[4], (TOKENS, 1), jnp.float32) ** block_scale(seeds[4], (TOKENS, 1), ((0, 64),), -0.2, 0.2), 0.1, 1.0)
    norm_gain = jnp.clip(1.0 + 0.15 * jax.random.normal(seeds[5], (D,), jnp.float32), 0.25, 1.75).astype(jnp.bfloat16)
    w_query = draw_w_query(jax.random.fold_in(seeds[9], 71), 0)
    w_key = draw_w_key(jax.random.fold_in(seeds[9], 71), 0)
    w_value = noise(seeds[8], (D, KVH * HD), D ** -0.5, 0.078125, ((1, 2),))
    return {"residual": residual, "shared_out": shared_out, "expert_out": expert_out, "routing": routing, "gate_score": gate_score, "norm_gain": norm_gain, "w_query": w_query, "w_key": w_key, "w_value": w_value}


ROPE_BASE = 500000.0
NORM_EPS = 1e-05
NEG_FILL = -1e+30

def token_positions(storage):
    half_block = TOK_DEV // 2
    device = storage // TOK_DEV
    within = storage % TOK_DEV
    early_pos = device * half_block + within
    late_pos = (2 * N_CTX - 1 - device) * half_block + (within - half_block)
    return jnp.where(within < half_block, early_pos, late_pos).astype(jnp.int32)

def storage_of(position):
    half_block = TOK_DEV // 2
    block_id = position // half_block
    offset = position % half_block
    device = jnp.where(block_id < N_CTX, block_id, 2 * N_CTX - 1 - block_id)
    within = jnp.where(block_id < N_CTX, offset, half_block + offset)
    return (device * TOK_DEV + within).astype(jnp.int32)

def rotate(projected, positions):
    row_count = projected.shape[0]
    head_count = projected.shape[1] // HD
    half_dim = HD // 2
    frequency = ROPE_BASE ** (-(jnp.arange(half_dim, dtype=jnp.float32) * 2.0 / HD))
    angles = positions.astype(jnp.float32)[:, None] * frequency[None, :]
    cos_part = jnp.cos(angles)[:, None, :]
    sin_part = jnp.sin(angles)[:, None, :]
    paired = projected.reshape(row_count, head_count, 2, half_dim)
    first_half = paired[:, :, 0, :]
    second_half = paired[:, :, 1, :]
    out_first = first_half * cos_part - second_half * sin_part
    out_second = second_half * cos_part + first_half * sin_part
    return jnp.stack([out_first, out_second], axis=2).reshape(row_count, head_count * HD)

def slot_numbers(expert_ids):
    row_count = expert_ids.shape[0]
    onehot = (expert_ids[:, None] == jnp.arange(EXPERTS, dtype=jnp.int32)[None, :]).astype(jnp.float32)
    earlier = (jnp.arange(row_count)[:, None] > jnp.arange(row_count)[None, :]).astype(jnp.float32)
    counts = jnp.dot(earlier, onehot, preferred_element_type=jnp.float32)
    return lax.optimization_barrier(jnp.sum(counts * onehot, axis=1)).astype(jnp.int32)

def reference(residual, shared_out, expert_out, routing, gate_score, norm_gain, w_query, w_key, w_value):
    expert_ids = routing[:, 0]
    slot_index = jax.vmap(slot_numbers)(expert_ids.reshape(N_CTX, TOK_DEV)).reshape(TOKENS)
    source = (jnp.arange(TOKENS, dtype=jnp.int32) // TOK_DEV).astype(jnp.int32)
    flat_index = ((expert_ids * N_CTX + source) * CAP + slot_index).astype(jnp.int32)
    picked = jnp.take(expert_out.reshape(EXPERTS * N_CTX * CAP, D), flat_index, axis=0)
    hidden_state = (residual.astype(jnp.float32) + shared_out.astype(jnp.float32) + gate_score * picked.astype(jnp.float32)).astype(jnp.bfloat16)
    wide = hidden_state.astype(jnp.float32)
    mean_square = lax.optimization_barrier(jnp.mean(wide * wide, axis=1, keepdims=True))
    normed = (wide * lax.rsqrt(mean_square + NORM_EPS) * norm_gain.astype(jnp.float32)).astype(jnp.bfloat16)
    positions = token_positions(jnp.arange(TOKENS, dtype=jnp.int32))
    queries = rotate(jnp.dot(normed, w_query, preferred_element_type=jnp.float32), positions).astype(jnp.bfloat16)
    keys_rot = rotate(jnp.dot(normed, w_key, preferred_element_type=jnp.float32), positions).astype(jnp.bfloat16)
    values = jnp.dot(normed, w_value, preferred_element_type=jnp.float32).astype(jnp.bfloat16)
    order = storage_of(jnp.arange(TOKENS, dtype=jnp.int32))
    group = QH // KVH
    block_len = min(512, TOKENS)
    block_count = TOKENS // block_len
    query_blocks = jnp.take(queries, order, axis=0).reshape(block_count, block_len, KVH, group, HD)
    key_blocks = jnp.take(keys_rot, order, axis=0).reshape(block_count, block_len, KVH, HD)
    value_blocks = jnp.take(values, order, axis=0).reshape(block_count, block_len, KVH, HD)
    scale = 1.0 / HD ** 0.5

    def one_block(block_index):
        query_here = lax.dynamic_index_in_dim(query_blocks, block_index, 0, keepdims=False).astype(jnp.float32)
        query_pos = block_index * block_len + jnp.arange(block_len)

        def advance(key_index, carry_state):
            running_max, denominator, weighted = carry_state
            key_here = lax.dynamic_index_in_dim(key_blocks, key_index, 0, keepdims=False).astype(jnp.float32)
            value_here = lax.dynamic_index_in_dim(value_blocks, key_index, 0, keepdims=False).astype(jnp.float32)
            key_pos = key_index * block_len + jnp.arange(block_len)
            scores = jnp.einsum('qhgd,khd->hgqk', query_here, key_here) * scale
            visible = key_pos[None, :] <= query_pos[:, None]
            scores = jnp.where(visible, scores, NEG_FILL)
            new_max = jnp.maximum(running_max, lax.optimization_barrier(jnp.max(scores, axis=-1)))
            weights_exp = jnp.where(visible, jnp.exp(scores - new_max[..., None]), 0.0)
            rescale = jnp.exp(running_max - new_max)
            denominator = denominator * rescale + lax.optimization_barrier(jnp.sum(weights_exp, axis=-1))
            rounded = lax.optimization_barrier(weights_exp.astype(jnp.bfloat16)).astype(jnp.float32)
            weighted = weighted * rescale[..., None] + jnp.einsum('hgqk,khd->hgqd', rounded, value_here)
            return (new_max, denominator, weighted)
        start_state = (jnp.full((KVH, group, block_len), NEG_FILL, jnp.float32), jnp.zeros((KVH, group, block_len), jnp.float32), jnp.zeros((KVH, group, block_len, HD), jnp.float32))
        running_max, denominator, weighted = lax.fori_loop(0, block_index + 1, advance, start_state)
        result = weighted / denominator[..., None]
        return jnp.transpose(result, (2, 0, 1, 3)).reshape(block_len, QH * HD).astype(jnp.bfloat16)
    natural = lax.map(one_block, jnp.arange(block_count)).reshape(TOKENS, QH * HD)
    attended = jnp.take(natural, positions, axis=0)
    return (hidden_state, attended)
```

```python
import functools
import math

import jax
import jax.numpy as jnp
from jax import lax
from jax.experimental import pallas as pl
from jax.experimental.pallas import tpu as pltpu
from jax.sharding import PartitionSpec as P

HD = 128
ROPE_BASE = 500000.0
NORM_EPS = 1e-05
NEG_FILL = -1e30
NY, NZ, NX, NK = 4, 2, 4, 2
GROUP = 5
HALF = 128
VMEM_LIMIT = 56 * 1024 * 1024


def split_index(c):
    return c // (NZ * NX * NK), (c // (NX * NK)) % NZ, (c // NK) % NX, c % NK


def join_index(y, z, x, k):
    return (((y % NY) * NZ + z % NZ) * NX + x % NX) * NK + k % NK


def permute(value, move):
    pairs = [(c, join_index(*move(*split_index(c)))) for c in range(NY * NZ * NX * NK)]
    return lax.ppermute(value, "ctx", pairs)


def core_swap(value):
    return permute(value, lambda y, z, x, k: (y, z, x, 1 - k))


def z_swap(value):
    return permute(value, lambda y, z, x, k: (y, 1 - z, x, k))


def first_axis(value, step):
    return permute(
        value, lambda y, z, x, k: (y, z, x - step, k) if k == 0 else (y - step, z, x, k)
    )


def second_axis(value, step):
    return permute(
        value, lambda y, z, x, k: (y - step, z, x, k) if k == 0 else (y, z, x - step, k)
    )


def params():
    return pltpu.CompilerParams(vmem_limit_bytes=VMEM_LIMIT)


def vmem():
    return pl.BlockSpec(memory_space=pltpu.VMEM)


def smem():
    return pl.BlockSpec(memory_space=pltpu.SMEM)


def pick_kernel(ids_col, ids_row, gate, returned, residual, shared, out, hot):
    @pl.when(pl.program_id(0) == 0)
    def _():
        rows = ids_col.shape[0]
        same = ids_col[...] == ids_row[...]
        row = lax.broadcasted_iota(jnp.int32, (rows, rows), 0)
        col = lax.broadcasted_iota(jnp.int32, (rows, rows), 1)
        slot = jnp.sum(jnp.where(same & (col < row), 1.0, 0.0), axis=1, keepdims=True)
        place = ids_col[...] * 4 + slot.astype(jnp.int32)
        lanes = lax.broadcasted_iota(jnp.int32, hot.shape, 1)
        hot[...] = jnp.where(lanes == place, 1.0, 0.0).astype(jnp.bfloat16)

    picked = jnp.dot(hot[...], returned[...], preferred_element_type=jnp.float32)
    total = residual[...].astype(jnp.float32) + shared[...].astype(jnp.float32)
    out[...] = (total + gate[...] * picked).astype(jnp.bfloat16)


def pick(ids, gate, returned, residual, shared):
    rows, width = residual.shape
    slots = returned.shape[0]
    block = 640
    wide = pl.BlockSpec((rows, block), lambda i: (0, i))
    return pl.pallas_call(
        pick_kernel,
        grid=(width // block,),
        in_specs=[
            pl.BlockSpec((rows, 1), lambda i: (0, 0)),
            pl.BlockSpec((1, rows), lambda i: (0, 0)),
            pl.BlockSpec((rows, 1), lambda i: (0, 0)),
            pl.BlockSpec((slots, block), lambda i: (0, i)),
            wide,
            wide,
        ],
        out_specs=wide,
        out_shape=jax.ShapeDtypeStruct((rows, width), jnp.bfloat16),
        scratch_shapes=[pltpu.VMEM((rows, slots), jnp.bfloat16)],
        compiler_params=params(),
        name="pick",
    )(ids, ids.reshape(1, rows), gate, returned, residual, shared)


def turn(x, cos, sin):
    return x * cos + pltpu.roll(x, HD // 2, 1) * sin


def key_value_kernel(h0, h1, gain, wk, wv, cos, sin, kv, normed):
    half = h0.shape[1]
    lo = h0[...].astype(jnp.float32)
    hi = h1[...].astype(jnp.float32)
    squares = jnp.sum(lo * lo, axis=1, keepdims=True) + jnp.sum(hi * hi, axis=1, keepdims=True)
    scale = lax.rsqrt(squares / (2 * half) + NORM_EPS)
    normed[:, :half] = (lo * scale * gain[:, :half].astype(jnp.float32)).astype(jnp.bfloat16)
    normed[:, half:] = (hi * scale * gain[:, half:].astype(jnp.float32)).astype(jnp.bfloat16)
    keys = jnp.dot(normed[...], wk[...], preferred_element_type=jnp.float32)
    values = jnp.dot(normed[...], wv[...], preferred_element_type=jnp.float32)
    for head in range(2):
        cols = slice(head * HD, (head + 1) * HD)
        kv[head, :, :HD] = turn(keys[:, cols], cos[...], sin[...]).astype(jnp.bfloat16)
        kv[head, :, HD:] = values[:, cols].astype(jnp.bfloat16)


def key_value(h0, h1, gain, wk, wv, cos, sin):
    rows, half = h0.shape
    return pl.pallas_call(
        key_value_kernel,
        in_specs=[vmem()] * 7,
        out_specs=[vmem()] * 2,
        out_shape=[
            jax.ShapeDtypeStruct((2, rows, 2 * HD), jnp.bfloat16),
            jax.ShapeDtypeStruct((rows, 2 * half), jnp.bfloat16),
        ],
        compiler_params=params(),
        cost_estimate=pl.CostEstimate(
            flops=2 * rows * 2 * half * 512, bytes_accessed=9_000_000, transcendentals=rows
        ),
        name="key_value",
    )(h0, h1, gain, wk, wv, cos, sin)


def query_kernel(factor, normed, wq, cos, sin, out):
    prod = jnp.dot(normed[...], wq[...], preferred_element_type=jnp.float32)
    for head in range(out.shape[0]):
        turned = turn(prod[:, head * HD : (head + 1) * HD], cos[...], sin[...])
        out[head] = (turned * factor).astype(jnp.bfloat16)


def query(normed, wq, cos, sin):
    rows, width = normed.shape
    heads = wq.shape[1] // HD
    per = 2
    factor = 1.0 / HD**0.5 * math.log2(math.e)
    return pl.pallas_call(
        functools.partial(query_kernel, factor),
        grid=(heads // per,),
        in_specs=[
            pl.BlockSpec((rows, width), lambda i: (0, 0)),
            pl.BlockSpec((width, per * HD), lambda i: (0, i)),
            pl.BlockSpec((rows, HD), lambda i: (0, 0)),
            pl.BlockSpec((rows, HD), lambda i: (0, 0)),
        ],
        out_specs=pl.BlockSpec((per, rows, HD), lambda i: (i, 0, 0)),
        out_shape=jax.ShapeDtypeStruct((heads, rows, HD), jnp.bfloat16),
        compiler_params=params(),
        cost_estimate=pl.CostEstimate(
            flops=2 * rows * width * heads * HD, bytes_accessed=17_000_000, transcendentals=0
        ),
        name="query",
    )(normed, wq, cos, sin)


def attend_kernel(counts, diag, resume, finish, *refs):
    flags, q, refs = refs[0], refs[1], refs[2:]
    kvs, refs = refs[: len(counts)], refs[len(counts) :]
    if resume:
        olds, refs = refs[:3], refs[3:]
    if finish:
        outs, (acc, den, top) = refs[:2], refs[2:]
    else:
        outs, (acc, den, top) = None, refs[:3]
    ones = jnp.ones((2 * HALF, HD), jnp.bfloat16)

    if resume:
        acc[...] = olds[0][...]
        den[...] = olds[1][...]
        top[...] = olds[2][...]
    else:
        acc[...] = jnp.zeros_like(acc)
        den[...] = jnp.zeros_like(den)
        top[...] = jnp.full_like(top, NEG_FILL)

    def rows_of(ref, lead, early, cols):
        at = pl.ds(early * HALF, HALF)
        if isinstance(lead, tuple):
            return jnp.concatenate([ref[0, lead[0], at, cols], ref[1, lead[0], at, cols]], axis=0)
        return jnp.concatenate([ref[lead, 0, at, cols], ref[lead, 1, at, cols]], axis=0)

    def update(side, head, keys, values, mask):
        query_rows = rows_of(q, (head,), side, slice(None))
        scores = lax.dot_general(
            query_rows, keys, (((1,), (1,)), ((), ())), preferred_element_type=jnp.float32
        )
        if mask is not None:
            scores = jnp.where(mask, scores, NEG_FILL)
        old = top[side, head]
        new = jnp.maximum(old, jnp.max(scores, axis=1, keepdims=True))
        weights = jnp.exp2(scores - new[:, :1]).astype(jnp.bfloat16)
        wide = jnp.concatenate([values, jnp.concatenate([ones] * (keys.shape[0] // ones.shape[0]))], axis=1)
        prod = jnp.dot(weights, wide, preferred_element_type=jnp.float32)
        keep = jnp.exp2(old - new)
        acc[side, head] = acc[side, head] * keep + prod[:, :HD]
        den[side, head] = den[side, head] * keep + prod[:, HD:]
        top[side, head] = new

    def per_head(head, carry):
        if diag:
            core = flags[0]
            row = lax.broadcasted_iota(jnp.int32, (2 * HALF, 2 * HALF), 0)
            col = lax.broadcasted_iota(jnp.int32, (2 * HALF, 2 * HALF), 1)
            for side in (0, 1):
                first = core if side == 0 else 1 - core
                row_pos = jnp.where(row < HALF, row + first * HALF, row - first * HALF)
                col_pos = jnp.where(col < HALF, col + first * HALF, col - first * HALF)
                update(
                    side,
                    head,
                    rows_of(kvs[0], 0, side, slice(0, HD)),
                    rows_of(kvs[0], 0, side, slice(HD, 2 * HD)),
                    col_pos <= row_pos,
                )
        start = 0
        for index, count in enumerate(counts):
            for base in range(0, count, 4):
                picks = range(base, min(base + 4, count))
                update(
                    1,
                    head,
                    jnp.concatenate([rows_of(kvs[index], b, 0, slice(0, HD)) for b in picks]),
                    jnp.concatenate([rows_of(kvs[index], b, 0, slice(HD, 2 * HD)) for b in picks]),
                    None,
                )
            for b in range(count):
                if diag and index == 0 and b == 0:
                    continue
                side = 1 - flags[start + b]
                update(
                    side,
                    head,
                    rows_of(kvs[index], b, side, slice(0, HD)),
                    rows_of(kvs[index], b, side, slice(HD, 2 * HD)),
                    None,
                )
            start += count
        return carry

    lax.fori_loop(0, GROUP, per_head, 0)

    if finish:
        part, logs = outs
        total = den[...]
        some = total > 0.0
        part[...] = jnp.where(some, acc[...] / jnp.where(some, total, 1.0), 0.0).astype(jnp.bfloat16)
        level = jnp.where(some, top[...] + jnp.log2(jnp.where(some, total, 1.0)), NEG_FILL)
        tiles = level.reshape(2 * GROUP * 2, HD, HD)
        row = lax.broadcasted_iota(jnp.int32, tiles.shape, 1)
        col = lax.broadcasted_iota(jnp.int32, tiles.shape, 2)
        logs[...] = jnp.sum(jnp.where(row == col, tiles, 0.0), axis=1)


STATE = (2, GROUP, 2 * HALF, HD)


def attend(flags, q, kvs, state, diag=False, finish=False):
    counts = tuple(kv.shape[0] for kv in kvs)
    state_shapes = [jax.ShapeDtypeStruct(STATE, jnp.float32)] * 3
    olds = [] if state is None else list(state)
    if finish:
        shapes = [
            jax.ShapeDtypeStruct(STATE, jnp.bfloat16),
            jax.ShapeDtypeStruct((4 * GROUP, HD), jnp.float32),
        ]
        scratch = [pltpu.VMEM(STATE, jnp.float32)] * 3
    else:
        shapes, scratch = state_shapes, []
    n = sum(counts)
    return pl.pallas_call(
        functools.partial(attend_kernel, counts, diag, state is not None, finish),
        in_specs=[smem()] + [vmem()] * (1 + len(kvs) + len(olds)),
        out_specs=[vmem()] * len(shapes),
        out_shape=shapes,
        scratch_shapes=scratch,
        compiler_params=params(),
        cost_estimate=pl.CostEstimate(
            flops=n * 2 * 1280 * 256 * 128 * 8,
            bytes_accessed=n * 262144 + 4_000_000,
            transcendentals=n * 2 * 1280 * 256,
        ),
        name="attend",
    )(flags, q, *kvs, *olds)


def merge_kernel(acc, den, top, part, logs, out):
    row = lax.broadcasted_iota(jnp.int32, (HD, HD), 0)
    col = lax.broadcasted_iota(jnp.int32, (HD, HD), 1)
    for side in range(2):
        for head in range(GROUP):
            for core in range(2):
                rows = slice(core * HALF, (core + 1) * HALF)
                total = den[side, head, rows]
                line = logs[pl.ds((side * GROUP + head) * 2 + core, 1), :]
                other = jnp.sum(jnp.where(row == col, line, 0.0), axis=1, keepdims=True)
                mine = top[side, head, rows] + jnp.log2(total)
                high = jnp.maximum(mine, other)
                first = jnp.exp2(mine - high)
                second = jnp.exp2(other - high)
                value = acc[side, head, rows] / total * first
                value = value + part[side, head, rows].astype(jnp.float32) * second
                out[core, side, :, head * HD : (head + 1) * HD] = (value / (first + second)).astype(
                    jnp.bfloat16
                )


def merge(state, part, logs):
    return pl.pallas_call(
        merge_kernel,
        in_specs=[vmem()] * 5,
        out_specs=vmem(),
        out_shape=jax.ShapeDtypeStruct((2, 2, HALF, GROUP * HD), jnp.bfloat16),
        compiler_params=params(),
        name="merge",
    )(*state, part, logs)


def rotations(ctx_index, rows):
    row = jnp.arange(rows, dtype=jnp.int32)
    half = rows // 2
    count = NY * NZ * NX * NK
    pos = jnp.where(row < half, ctx_index * half + row, (2 * count - 1 - ctx_index) * half + row - half)
    frequency = ROPE_BASE ** (-(jnp.arange(HD // 2, dtype=jnp.float32) * 2.0 / HD))
    angles = pos.astype(jnp.float32)[:, None] * frequency[None, :]
    cos, sin = jnp.cos(angles), jnp.sin(angles)
    return jnp.concatenate([cos, cos], axis=1), jnp.concatenate([-sin, sin], axis=1)


def chip_order(y, z, x):
    return (y * NZ + z) * NX + x


def shards(residual, shared_out, expert_out, routing, gate_score, norm_gain, w_query, w_key, w_value):
    rows, half_width = residual.shape
    ctx_index = lax.axis_index("ctx")
    tp_index = lax.axis_index("tp")
    y, z, x, k = split_index(ctx_index)
    cos, sin = rotations(ctx_index, rows)

    own_experts, sources, slots, _ = expert_out.shape
    outgoing = jnp.transpose(expert_out, (1, 0, 2, 3)).reshape(sources, own_experts * slots, half_width)
    returned = lax.all_to_all(outgoing, "ctx", split_axis=0, concat_axis=0, tiled=True)
    returned = returned.reshape(sources * own_experts * slots, half_width)
    hidden = pick(routing, gate_score, returned, residual, shared_out)

    other = lax.ppermute(hidden, "tp", [(0, 1), (1, 0)])
    h0 = jnp.where(tp_index == 0, hidden, other)
    h1 = jnp.where(tp_index == 0, other, hidden)
    kv, normed = key_value(h0, h1, norm_gain.reshape(1, -1), w_key, w_value, cos, sin)
    kv_mine = lax.dynamic_index_in_dim(kv, k, 0, keepdims=False)
    kv_other = lax.dynamic_index_in_dim(kv, 1 - k, 0, keepdims=False)
    block = jnp.stack([kv_mine, core_swap(kv_other)])[None]

    near = [first_axis(block, step) for step in (1, -1, 2)]

    queries = query(normed, w_query, cos, sin).reshape(2, GROUP, rows, HD)
    q_mine = lax.dynamic_index_in_dim(queries, k, 0, keepdims=False)
    q_other = lax.dynamic_index_in_dim(queries, 1 - k, 0, keepdims=False)
    q_own = jnp.stack([q_mine, core_swap(q_other)])
    q_pair = z_swap(q_own)

    line = jnp.concatenate([block] + near)
    far = [second_axis(line, step) for step in (1, -1, 2)]

    steps = jnp.array([0, 1, -1, 2], jnp.int32)

    def before(first, second, chip):
        by = jnp.where(k == 0, second, first)
        bx = jnp.where(k == 0, first, second)
        return (chip_order((y + by) % NY, z, (x + bx) % NX) < chip).astype(jnp.int32)

    own_chip = chip_order(y, z, x)
    pair_chip = chip_order(y, 1 - z, x)
    zero = jnp.zeros((4,), jnp.int32)
    own_near = before(steps, zero, own_chip).at[0].set(k)
    pair_near = before(steps, zero, pair_chip)
    own_far = jnp.concatenate([before(steps, zero + s, own_chip) for s in (1, -1, 2)])
    pair_far = jnp.concatenate([before(steps, zero + s, pair_chip) for s in (1, -1, 2)])

    own_state = attend(own_near, q_own, [line], None, diag=True)
    pair_state = attend(pair_near, q_pair, [line], None)
    pair_state = attend(pair_far[:8], q_pair, far[:2], pair_state)
    part, logs = attend(pair_far[8:], q_pair, far[2:], pair_state, finish=True)
    part = z_swap(part)
    logs = z_swap(logs)
    own_state = attend(own_far, q_own, far, own_state)
    out = merge(own_state, part, logs)
    keep = lax.dynamic_index_in_dim(out, 0, 0, keepdims=False).reshape(rows, GROUP * HD)
    sent = core_swap(out[1].reshape(rows, GROUP * HD))
    attended = jnp.where(
        k == 0,
        jnp.concatenate([keep, sent], axis=1),
        jnp.concatenate([sent, keep], axis=1),
    )
    return hidden, attended


def solution(mesh):
    return jax.shard_map(
        shards,
        mesh=mesh,
        in_specs=(
            P("ctx", "tp"),
            P("ctx", "tp"),
            P("ctx", None, None, "tp"),
            P("ctx", None),
            P("ctx", None),
            P(),
            P(None, "tp"),
            P(None, "tp"),
            P(None, "tp"),
        ),
        out_specs=(P("ctx", "tp"), P("ctx", "tp")),
        check_vma=False,
    )
```

```python
import functools
import math

import jax
import jax.numpy as jnp
from jax import lax
from jax.experimental import pallas as pl
from jax.experimental.pallas import tpu as pltpu
from jax.sharding import PartitionSpec as P

HD = 128
ROPE_BASE = 500000.0
NORM_EPS = 1e-05
NEG_FILL = -1e30
NY, NZ, NX, NK = 4, 2, 4, 2
GROUP = 5
HALF = 128
def split_index(c):
    return c // (NZ * NX * NK), (c // (NX * NK)) % NZ, (c // NK) % NX, c % NK


def join_index(y, z, x, k):
    return (((y % NY) * NZ + z % NZ) * NX + x % NX) * NK + k % NK


def permute(value, move):
    pairs = [(c, join_index(*move(*split_index(c)))) for c in range(NY * NZ * NX * NK)]
    return lax.ppermute(value, "ctx", pairs)


def core_swap(value):
    return permute(value, lambda y, z, x, k: (y, z, x, 1 - k))


def z_swap(value):
    return permute(value, lambda y, z, x, k: (y, 1 - z, x, k))


def first_axis(value, step):
    return permute(
        value, lambda y, z, x, k: (y, z, x - step, k) if k == 0 else (y - step, z, x, k)
    )


def second_axis(value, step):
    return permute(
        value, lambda y, z, x, k: (y - step, z, x, k) if k == 0 else (y, z, x - step, k)
    )


def params(mib=24):
    return pltpu.CompilerParams(vmem_limit_bytes=mib * 1024 * 1024)


def vmem():
    return pl.BlockSpec(memory_space=pltpu.VMEM)


def smem():
    return pl.BlockSpec(memory_space=pltpu.SMEM)


def choose_kernel(ids_col, ids_row, hot):
    rows = ids_col.shape[0]
    same = ids_col[...] == ids_row[...]
    row = lax.broadcasted_iota(jnp.int32, (rows, rows), 0)
    col = lax.broadcasted_iota(jnp.int32, (rows, rows), 1)
    slot = jnp.sum(jnp.where(same & (col < row), 1.0, 0.0), axis=1, keepdims=True)
    place = ids_col[...] * 4 + slot.astype(jnp.int32)
    lanes = lax.broadcasted_iota(jnp.int32, hot.shape, 1)
    hot[...] = jnp.where(lanes == place, 1.0, 0.0).astype(jnp.bfloat16)


def choose(ids, slots):
    rows = ids.shape[0]
    return pl.pallas_call(
        choose_kernel,
        in_specs=[vmem()] * 2,
        out_specs=vmem(),
        out_shape=jax.ShapeDtypeStruct((rows, slots), jnp.bfloat16),
        compiler_params=params(),
        cost_estimate=pl.CostEstimate(flops=2_000_000, bytes_accessed=600_000, transcendentals=0),
        name="choose",
    )(ids, ids.reshape(1, rows))


def pick_kernel(hot, gate, returned, residual, shared, out):
    picked = jnp.dot(hot[...], returned[...], preferred_element_type=jnp.float32)
    total = residual[...].astype(jnp.float32) + shared[...].astype(jnp.float32)
    out[...] = (total + gate[...] * picked).astype(jnp.bfloat16)


def pick(hot, gate, returned, residual, shared):
    rows, width = residual.shape
    slots = returned.shape[0]
    block = 640
    wide = pl.BlockSpec((rows, block), lambda i: (0, i))
    return pl.pallas_call(
        pick_kernel,
        grid=(width // block,),
        in_specs=[
            pl.BlockSpec((rows, slots), lambda i: (0, 0)),
            pl.BlockSpec((rows, 1), lambda i: (0, 0)),
            pl.BlockSpec((slots, block), lambda i: (0, i)),
            wide,
            wide,
        ],
        out_specs=wide,
        out_shape=jax.ShapeDtypeStruct((rows, width), jnp.bfloat16),
        compiler_params=params(),
        name="pick",
    )(hot, gate, returned, residual, shared)


def turn(x, cos, sin):
    return x * cos + pltpu.roll(x, HD // 2, 1) * sin


def gained(h, gain):
    return (h.astype(jnp.float32) * gain[0].astype(jnp.float32)).astype(jnp.bfloat16)


def key_value_first_kernel(tp, h, gain, wk, wv, part, squares):
    wide = h[...].astype(jnp.float32)
    squares[...] = jnp.sum(wide * wide, axis=1, keepdims=True)
    x = gained(h[...], gain[...])
    part[:, : 2 * HD] = jnp.dot(x, wk[...], preferred_element_type=jnp.float32)
    part[:, 2 * HD :] = jnp.dot(x, wv[...], preferred_element_type=jnp.float32)


def half_specs(rows, half, other, blocks):
    def of(tp):
        return 1 - tp[0] if other else tp[0]

    return [
        pl.BlockSpec((rows, half), lambda i, tp: (0, 0)),
        pl.BlockSpec((1, 1, half), lambda i, tp: (of(tp), 0, 0)),
    ] + [pl.BlockSpec((half, cols), lambda i, tp: (of(tp), i)) for cols in blocks]


def whole(*shape):
    return pl.BlockSpec(shape, lambda i, tp: (0,) * len(shape))


def projection_cost(rows, half, cols):
    return pl.CostEstimate(
        flops=2 * rows * half * cols,
        bytes_accessed=2 * half * cols + 2 * rows * half + 4 * rows * cols,
        transcendentals=0,
    )


def key_value_first(tp, h, gain, wk, wv):
    rows, half = h.shape
    cols = wk.shape[1]
    return pl.pallas_call(
        key_value_first_kernel,
        grid_spec=pltpu.PrefetchScalarGridSpec(
            num_scalar_prefetch=1,
            grid=(1,),
            in_specs=half_specs(rows, half, False, (cols, cols)),
            out_specs=[whole(rows, 2 * cols), whole(rows, 1)],
        ),
        out_shape=[
            jax.ShapeDtypeStruct((rows, 2 * cols), jnp.float32),
            jax.ShapeDtypeStruct((rows, 1), jnp.float32),
        ],
        compiler_params=params(),
        cost_estimate=projection_cost(rows, half, 2 * cols),
        name="key_value_first",
    )(tp, h, gain, wk, wv)


def key_value_kernel(tp, h, gain, wk, wv, part, squares, cos, sin, kv, scale):
    half = h.shape[1]
    wide = h[...].astype(jnp.float32)
    total = squares[...] + jnp.sum(wide * wide, axis=1, keepdims=True)
    factor = lax.rsqrt(total / (2 * half) + NORM_EPS)
    scale[...] = factor
    x = gained(h[...], gain[...])
    keys = part[:, : 2 * HD] + jnp.dot(x, wk[...], preferred_element_type=jnp.float32)
    values = part[:, 2 * HD :] + jnp.dot(x, wv[...], preferred_element_type=jnp.float32)
    for head in range(2):
        cols = slice(head * HD, (head + 1) * HD)
        turned = turn(keys[:, cols] * factor, cos[...], sin[...]).astype(jnp.bfloat16)
        value = (values[:, cols] * factor).T.astype(jnp.bfloat16)
        for side in range(2):
            rows = slice(side * HALF, (side + 1) * HALF)
            kv[head, side, 0] = turned[rows]
            kv[head, side, 1] = value[:, rows]


def key_value(tp, h, gain, wk, wv, part, squares, cos, sin):
    rows, half = h.shape
    cols = wk.shape[1]
    return pl.pallas_call(
        key_value_kernel,
        grid_spec=pltpu.PrefetchScalarGridSpec(
            num_scalar_prefetch=1,
            grid=(1,),
            in_specs=half_specs(rows, half, True, (cols, cols))
            + [whole(rows, 2 * cols), whole(rows, 1), whole(rows, HD), whole(rows, HD)],
            out_specs=[whole(2, 2, 2, HALF, HD), whole(rows, 1)],
        ),
        out_shape=[
            jax.ShapeDtypeStruct((2, 2, 2, HALF, HD), jnp.bfloat16),
            jax.ShapeDtypeStruct((rows, 1), jnp.float32),
        ],
        compiler_params=params(),
        cost_estimate=projection_cost(rows, half, 2 * cols),
        name="key_value",
    )(tp, h, gain, wk, wv, part, squares, cos, sin)


def query_first_kernel(tp, h, gain, wq, part, x):
    @pl.when(pl.program_id(0) == 0)
    def _():
        x[...] = gained(h[...], gain[...])

    part[...] = jnp.dot(x[...], wq[...], preferred_element_type=jnp.float32)


def query_first(tp, h, gain, wq):
    rows, half = h.shape
    cols, block = wq.shape[1], 2 * HD
    return pl.pallas_call(
        query_first_kernel,
        grid_spec=pltpu.PrefetchScalarGridSpec(
            num_scalar_prefetch=1,
            grid=(cols // block,),
            in_specs=half_specs(rows, half, False, (block,)),
            out_specs=pl.BlockSpec((rows, block), lambda i, tp: (0, i)),
            scratch_shapes=[pltpu.VMEM((rows, half), jnp.bfloat16)],
        ),
        out_shape=jax.ShapeDtypeStruct((rows, cols), jnp.float32),
        compiler_params=params(),
        cost_estimate=projection_cost(rows, half, cols),
        name="query_first",
    )(tp, h, gain, wq)


def query_kernel(tp, h, gain, wq, part, scale, cos, sin, out, x):
    @pl.when(pl.program_id(0) == 0)
    def _():
        x[...] = gained(h[...], gain[...])

    prod = part[...] + jnp.dot(x[...], wq[...], preferred_element_type=jnp.float32)
    prod = prod * (scale[...] * (1.0 / HD**0.5 * math.log2(math.e)))
    for head in range(2):
        turned = turn(prod[:, head * HD : (head + 1) * HD], cos[...], sin[...]).T.astype(jnp.bfloat16)
        for side in range(2):
            out[head, side] = turned[:, side * HALF : (side + 1) * HALF]


def query(tp, h, gain, wq, part, scale, cos, sin):
    rows, half = h.shape
    cols, block = wq.shape[1], 2 * HD
    return pl.pallas_call(
        query_kernel,
        grid_spec=pltpu.PrefetchScalarGridSpec(
            num_scalar_prefetch=1,
            grid=(cols // block,),
            in_specs=half_specs(rows, half, True, (block,))
            + [
                pl.BlockSpec((rows, block), lambda i, tp: (0, i)),
                whole(rows, 1),
                whole(rows, HD),
                whole(rows, HD),
            ],
            out_specs=pl.BlockSpec((2, 2, HD, HALF), lambda i, tp: (i, 0, 0, 0)),
            scratch_shapes=[pltpu.VMEM((rows, half), jnp.bfloat16)],
        ),
        out_shape=jax.ShapeDtypeStruct((cols // HD, 2, HD, HALF), jnp.bfloat16),
        compiler_params=params(),
        cost_estimate=projection_cost(rows, half, cols),
        name="query",
    )(tp, h, gain, wq, part, scale, cos, sin)


ONES = 16


def attend_kernel(counts, diag, resume, finish, *refs):
    flags, q, refs = refs[0], refs[1], refs[2:]
    kvs, refs = refs[: len(counts)], refs[len(counts) :]
    olds = refs[:3] if resume else ()
    refs = refs[len(olds) :]
    part = logs = None
    if finish:
        part, logs, refs = refs[0], refs[1], refs[2:]
    acc, den, top, klist, vlist = refs
    total = klist.shape[0]

    if resume:
        acc[...] = olds[0][...]
        den[...] = olds[1][...]
        top[...] = olds[2][...]
    else:
        acc[...] = jnp.zeros_like(acc)
        den[...] = jnp.zeros_like(den)
        top[...] = jnp.full_like(top, NEG_FILL)

    vlist[:, HD:, :] = jnp.ones((total, ONES, 2 * HALF), jnp.bfloat16)

    def put(place, kv, block, side):
        for core in range(2):
            span = slice(core * HALF, (core + 1) * HALF)
            klist[place, span, :] = kv[block, core, side, 0]
            vlist[place, :HD, span] = kv[block, core, side, 1]

    last = total - 2 if diag else total - 1
    front, back = jnp.int32(0), jnp.int32(last)
    start = 0
    for kv, count in zip(kvs, counts):
        for block in range(count):
            put(front, kv, block, 0)
            front = front + 1
            if diag and start + block == 0:
                continue
            early = flags[start + block]
            put(jnp.where(early == 1, back, front), kv, block, 1 - early)
            front = front + 1 - early
            back = back - early
        start += count
    n_late = front
    n_early = last - back

    def update(side, places, mask):
        keys = jnp.concatenate([klist[p] for p in places], axis=0)
        scores = []
        for head in range(GROUP):
            columns = jnp.concatenate([q[0, head, side], q[1, head, side]], axis=1)
            scores.append(jnp.dot(keys, columns, preferred_element_type=jnp.float32))
        values = jnp.concatenate([vlist[p] for p in places], axis=1)
        for head in range(GROUP):
            s = scores[head]
            if mask is not None:
                s = jnp.where(mask, s, NEG_FILL)
            old = top[side, head]
            new = jnp.maximum(old, jnp.max(s, axis=0, keepdims=True))
            weights = jnp.exp2(s - new[:1]).astype(jnp.bfloat16)
            prod = jnp.dot(values, weights, preferred_element_type=jnp.float32)
            keep = jnp.exp2(old - new)
            acc[side, head] = acc[side, head] * keep[:1] + prod[:HD]
            den[side, head] = den[side, head] * keep + prod[HD : HD + 8]
            top[side, head] = new

    if diag:
        core = flags[0]
        row = lax.broadcasted_iota(jnp.int32, (2 * HALF, 2 * HALF), 0)
        col = lax.broadcasted_iota(jnp.int32, (2 * HALF, 2 * HALF), 1)

        def own(side, carry):
            first = jnp.where(side == 0, core, 1 - core)
            key_pos = jnp.where(row < HALF, row + first * HALF, row - first * HALF)
            query_pos = jnp.where(col < HALF, col + first * HALF, col - first * HALF)
            put(total - 1, kvs[0], 0, side)
            update(side, (total - 1,), key_pos <= query_pos)
            return carry

        lax.fori_loop(0, 2, own, 0)

    pairs = n_late // 2
    early_pairs = n_early // 2
    def two(i, carry):
        late = i < pairs
        j = i - pairs
        one = jnp.where(late, 2 * i, last - 2 * j)
        other = jnp.where(late, 2 * i + 1, last - 2 * j - 1)
        update(jnp.where(late, 1, 0), (one, other), None)
        return carry

    lax.fori_loop(0, pairs + early_pairs, two, 0)
    odd_late = n_late - 2 * pairs
    odd_early = n_early - 2 * early_pairs

    def one(i, carry):
        late = i < odd_late
        update(jnp.where(late, 1, 0), (jnp.where(late, n_late - 1, last - n_early + 1),), None)
        return carry

    lax.fori_loop(0, odd_late + odd_early, one, 0)

    if finish:
        for side in range(2):
            for head in range(GROUP):
                denominator = den[side, head]
                some = denominator > 0.0
                safe = jnp.where(some, denominator, 1.0)
                inverse = jnp.where(some, 1.0 / safe, 0.0)
                part[side, head] = (acc[side, head] * inverse[:1]).astype(jnp.bfloat16)
                level = jnp.where(some, top[side, head] + jnp.log2(safe), NEG_FILL)
                place = side * GROUP + head
                logs[place : place + 1, :] = level[:1]


ACC = (2, GROUP, HD, 2 * HALF)
ROWS = (2, GROUP, 8, 2 * HALF)


def attend(flags, q, kvs, state, diag=False, finish=False):
    counts = tuple(kv.shape[0] for kv in kvs)
    n = sum(counts)
    total = 2 * n
    olds = [] if state is None else list(state)
    states = (ACC, ROWS, ROWS)
    scratch = [
        pltpu.VMEM((total, 2 * HALF, HD), jnp.bfloat16),
        pltpu.VMEM((total, HD + ONES, 2 * HALF), jnp.bfloat16),
    ]
    if finish:
        shapes = [
            jax.ShapeDtypeStruct(ACC, jnp.bfloat16),
            jax.ShapeDtypeStruct((2 * GROUP, 2 * HALF), jnp.float32),
        ]
        scratch = [pltpu.VMEM(shape, jnp.float32) for shape in states] + scratch
    else:
        shapes = [jax.ShapeDtypeStruct(shape, jnp.float32) for shape in states]
    return pl.pallas_call(
        functools.partial(attend_kernel, counts, diag, state is not None, finish),
        in_specs=[smem()] + [vmem()] * (1 + len(kvs) + len(olds)),
        out_specs=[vmem()] * len(shapes),
        out_shape=shapes,
        scratch_shapes=scratch,
        compiler_params=params(),
        cost_estimate=pl.CostEstimate(
            flops=n * 2 * 1280 * 256 * 128 * 8,
            bytes_accessed=n * 262144 + 4_000_000,
            transcendentals=n * 2 * 1280 * 256,
        ),
        name="attend",
    )(flags, q, *kvs, *olds)


def merge_kernel(acc, den, top, part, logs, out):
    for side in range(2):
        for head in range(GROUP):
            place = side * GROUP + head
            total = den[side, head][:1]
            other = logs[place : place + 1, :]
            mine = top[side, head][:1] + jnp.log2(total)
            high = jnp.maximum(mine, other)
            first = jnp.exp2(mine - high)
            second = jnp.exp2(other - high)
            weight = 1.0 / (first + second)
            value = acc[side, head] * (first * weight / total)
            value = value + part[side, head].astype(jnp.float32) * (second * weight)
            rows = value.T.astype(jnp.bfloat16)
            for core in range(2):
                out[core, side, :, head * HD : (head + 1) * HD] = rows[core * HALF : (core + 1) * HALF]


def merge(state, part, logs):
    return pl.pallas_call(
        merge_kernel,
        in_specs=[vmem()] * 5,
        out_specs=vmem(),
        out_shape=jax.ShapeDtypeStruct((2, 2, HALF, GROUP * HD), jnp.bfloat16),
        compiler_params=params(),
        name="merge",
    )(*state, part, logs)


def rotations(ctx_index, rows):
    row = jnp.arange(rows, dtype=jnp.int32)
    half = rows // 2
    count = NY * NZ * NX * NK
    pos = jnp.where(row < half, ctx_index * half + row, (2 * count - 1 - ctx_index) * half + row - half)
    frequency = ROPE_BASE ** (-(jnp.arange(HD // 2, dtype=jnp.float32) * 2.0 / HD))
    angles = pos.astype(jnp.float32)[:, None] * frequency[None, :]
    cos, sin = jnp.cos(angles), jnp.sin(angles)
    return jnp.concatenate([cos, cos], axis=1), jnp.concatenate([-sin, sin], axis=1)


def chip_order(y, z, x):
    return (y * NZ + z) * NX + x


def shards(residual, shared_out, expert_out, routing, gate_score, norm_gain, w_query, w_key, w_value):
    rows, half_width = residual.shape
    ctx_index = lax.axis_index("ctx")
    tp_index = lax.axis_index("tp")
    y, z, x, k = split_index(ctx_index)
    cos, sin = rotations(ctx_index, rows)

    own_experts, sources, slots, _ = expert_out.shape
    outgoing = jnp.transpose(expert_out, (1, 0, 2, 3)).reshape(sources, own_experts * slots, half_width)
    returned = lax.all_to_all(outgoing, "ctx", split_axis=0, concat_axis=0, tiled=True)
    returned = returned.reshape(sources * own_experts * slots, half_width)
    hidden = pick(choose(routing, returned.shape[0]), gate_score, returned, residual, shared_out)

    other = lax.ppermute(hidden, "tp", [(0, 1), (1, 0)])
    tp = tp_index.reshape(1)
    gain = norm_gain.reshape(2, 1, half_width)
    kv_part, squares = key_value_first(tp, hidden, gain, w_key, w_value)
    query_part = query_first(tp, hidden, gain, w_query)
    kv, scale = key_value(tp, other, gain, w_key, w_value, kv_part, squares, cos, sin)
    kv_mine = lax.dynamic_index_in_dim(kv, k, 0, keepdims=False)
    kv_other = lax.dynamic_index_in_dim(kv, 1 - k, 0, keepdims=False)
    block = jnp.stack([kv_mine, core_swap(kv_other)])[None]

    near = [first_axis(block, step) for step in (1, -1, 2)]

    queries = query(tp, other, gain, w_query, query_part, scale, cos, sin)
    queries = queries.reshape(2, GROUP, 2, HD, HALF)
    q_mine = lax.dynamic_index_in_dim(queries, k, 0, keepdims=False)
    q_other = lax.dynamic_index_in_dim(queries, 1 - k, 0, keepdims=False)
    q_own = jnp.stack([q_mine, core_swap(q_other)])
    q_pair = z_swap(q_own)

    line = jnp.concatenate([block] + near)
    far = [second_axis(line, step) for step in (1, -1, 2)]

    steps = jnp.array([0, 1, -1, 2], jnp.int32)

    def before(first, second, chip):
        by = jnp.where(k == 0, second, first)
        bx = jnp.where(k == 0, first, second)
        return (chip_order((y + by) % NY, z, (x + bx) % NX) < chip).astype(jnp.int32)

    own_chip = chip_order(y, z, x)
    pair_chip = chip_order(y, 1 - z, x)
    zero = jnp.zeros((4,), jnp.int32)
    own_near = before(steps, zero, own_chip).at[0].set(k)
    pair_near = before(steps, zero, pair_chip)
    own_far = jnp.concatenate([before(steps, zero + s, own_chip) for s in (1, -1, 2)])
    pair_far = jnp.concatenate([before(steps, zero + s, pair_chip) for s in (1, -1, 2)])

    own_state = attend(own_near, q_own, [line], None, diag=True)
    pair_state = attend(pair_near, q_pair, [line], None)
    pair_state = attend(pair_far[:8], q_pair, far[:2], pair_state)
    part, logs = attend(pair_far[8:], q_pair, far[2:], pair_state, finish=True)
    part = z_swap(part)
    logs = z_swap(logs)
    own_state = attend(own_far, q_own, far, own_state)
    out = merge(own_state, part, logs)
    keep = lax.dynamic_index_in_dim(out, 0, 0, keepdims=False).reshape(rows, GROUP * HD)
    sent = core_swap(out[1].reshape(rows, GROUP * HD))
    attended = jnp.where(
        k == 0,
        jnp.concatenate([keep, sent], axis=1),
        jnp.concatenate([sent, keep], axis=1),
    )
    return hidden, attended


def solution(mesh):
    return jax.shard_map(
        shards,
        mesh=mesh,
        in_specs=(
            P("ctx", "tp"),
            P("ctx", "tp"),
            P("ctx", None, None, "tp"),
            P("ctx", None),
            P("ctx", None),
            P(),
            P(None, "tp"),
            P(None, "tp"),
            P(None, "tp"),
        ),
        out_specs=(P("ctx", "tp"), P("ctx", "tp")),
        check_vma=False,
    )
```

```python
import functools
import math

import jax
import jax.numpy as jnp
from jax import lax
from jax.experimental import pallas as pl
from jax.experimental.pallas import tpu as pltpu
from jax.sharding import PartitionSpec as P

HD = 128
ROPE_BASE = 500000.0
NORM_EPS = 1e-05
NEG_FILL = -1e30
NY, NZ, NX, NK = 4, 2, 4, 2
GROUP = 5
HALF = 128
ALONE = 60
def split_index(c):
    return c // (NZ * NX * NK), (c // (NX * NK)) % NZ, (c // NK) % NX, c % NK


def join_index(y, z, x, k):
    return (((y % NY) * NZ + z % NZ) * NX + x % NX) * NK + k % NK


def permute(value, move):
    pairs = [(c, join_index(*move(*split_index(c)))) for c in range(NY * NZ * NX * NK)]
    return lax.ppermute(value, "ctx", pairs)


def core_swap(value):
    return permute(value, lambda y, z, x, k: (y, z, x, 1 - k))


def to_pair(value):
    return permute(value, lambda y, z, x, k: (y, 1 - z, x, k))


def to_pair_other(value):
    return permute(value, lambda y, z, x, k: (y, 1 - z, x, 1 - k))


def first_axis(value, step):
    return permute(
        value, lambda y, z, x, k: (y, z, x - step, k) if k == 0 else (y - step, z, x, k)
    )


def second_axis(value, step):
    return permute(
        value, lambda y, z, x, k: (y - step, z, x, k) if k == 0 else (y, z, x - step, k)
    )


def params(mib=24):
    return pltpu.CompilerParams(vmem_limit_bytes=mib * 1024 * 1024)


def takes(microseconds):
    return pl.CostEstimate(flops=int(microseconds * 1.15e9), bytes_accessed=0, transcendentals=0)


def vmem():
    return pl.BlockSpec(memory_space=pltpu.VMEM)


def anywhere():
    return pl.BlockSpec(memory_space=pl.ANY)


def hbm():
    return pl.BlockSpec(memory_space=pltpu.HBM)


def smem():
    return pl.BlockSpec(memory_space=pltpu.SMEM)


def choose_kernel(ids_col, ids_row, hot):
    rows = ids_col.shape[0]
    same = ids_col[...] == ids_row[...]
    row = lax.broadcasted_iota(jnp.int32, (rows, rows), 0)
    col = lax.broadcasted_iota(jnp.int32, (rows, rows), 1)
    slot = jnp.sum(jnp.where(same & (col < row), 1.0, 0.0), axis=1, keepdims=True)
    place = ids_col[...] * 4 + slot.astype(jnp.int32)
    lanes = lax.broadcasted_iota(jnp.int32, hot.shape, 1)
    hot[...] = jnp.where(lanes == place, 1.0, 0.0).astype(jnp.bfloat16)


def choose(ids, slots):
    rows = ids.shape[0]
    return pl.pallas_call(
        choose_kernel,
        in_specs=[vmem()] * 2,
        out_specs=vmem(),
        out_shape=jax.ShapeDtypeStruct((rows, slots), jnp.bfloat16),
        compiler_params=params(),
        cost_estimate=pl.CostEstimate(flops=2_000_000, bytes_accessed=600_000, transcendentals=0),
        name="choose",
    )(ids, ids.reshape(1, rows))


def relayout_kernel(experts, out, loaded, ready, arrive, leave):
    chunks, slots = loaded.shape[0], experts.shape[2]
    group = loaded.shape[2]

    def load(i):
        return pltpu.make_async_copy(experts.at[:, pl.ds(i * group, group)], loaded.at[i], arrive.at[i])

    def store(i):
        return pltpu.make_async_copy(ready.at[i], out.at[pl.ds(i * group, group)], leave.at[i])

    for i in range(chunks):
        load(i).start()
    for i in range(chunks):
        load(i).wait()
        for expert in range(experts.shape[0]):
            ready[i, :, expert * slots : (expert + 1) * slots, :] = loaded[i, expert]
        store(i).start()
    for i in range(chunks):
        store(i).wait()


def relayout(expert_out):
    experts, sources, slots, width = expert_out.shape
    chunks = 8
    group = sources // chunks
    return pl.pallas_call(
        relayout_kernel,
        in_specs=[anywhere()],
        out_specs=anywhere(),
        out_shape=jax.ShapeDtypeStruct((sources, experts * slots, width), jnp.bfloat16),
        scratch_shapes=[
            pltpu.VMEM((chunks, experts, group, slots, width), jnp.bfloat16),
            pltpu.VMEM((chunks, group, experts * slots, width), jnp.bfloat16),
            pltpu.SemaphoreType.DMA((chunks,)),
            pltpu.SemaphoreType.DMA((chunks,)),
        ],
        compiler_params=params(ALONE),
        name="relayout",
    )(expert_out)


def pick_kernel(first, hot, gate, returned, residual, shared, after, out, base, extra, done, arrive, leave):
    chunks, block, width = base.shape
    cols = slice(first, first + width)

    def loads(i):
        rows = pl.ds(i * block, block)
        return [
            pltpu.make_async_copy(residual.at[rows, cols], base.at[i], arrive.at[0, i]),
            pltpu.make_async_copy(shared.at[rows, cols], extra.at[i], arrive.at[1, i]),
        ]

    def store(i):
        return pltpu.make_async_copy(done.at[i], out.at[pl.ds(i * block, block)], leave.at[i])

    for i in range(chunks):
        for copy in loads(i):
            copy.start()
    for i in range(chunks):
        rows = slice(i * block, (i + 1) * block)
        picked = jnp.dot(hot[rows], returned[:, cols], preferred_element_type=jnp.float32)
        for copy in loads(i):
            copy.wait()
        total = base[i].astype(jnp.float32) + extra[i].astype(jnp.float32)
        done[i] = (total + gate[rows] * picked).astype(jnp.bfloat16)
        store(i).start()
    for i in range(chunks):
        store(i).wait()


def pick(part, hot, gate, returned, residual, shared, after):
    rows, width = residual.shape
    width = width // 2
    chunks = 2
    tile = pltpu.VMEM((chunks, rows // chunks, width), jnp.bfloat16)
    return pl.pallas_call(
        functools.partial(pick_kernel, part * width),
        in_specs=[vmem()] * 3 + [hbm()] * 2 + [anywhere()],
        out_specs=hbm(),
        out_shape=jax.ShapeDtypeStruct((rows, width), jnp.bfloat16),
        scratch_shapes=[
            tile,
            tile,
            tile,
            pltpu.SemaphoreType.DMA((2, chunks)),
            pltpu.SemaphoreType.DMA((chunks,)),
        ],
        compiler_params=params(10),
        cost_estimate=takes(2.5),
        name="pick",
    )(hot, gate, returned, residual, shared, after)


KV_TILES, Q_TILES = 4, 2 * GROUP


def turn(x, cos, sin):
    return x * cos + pltpu.roll(x, HD // 2, 1) * sin


def gained(h, gain):
    return (h.astype(jnp.float32) * gain.astype(jnp.float32)).astype(jnp.bfloat16)


def squared(h):
    wide = h.astype(jnp.float32)
    return jnp.sum(wide * wide, axis=1, keepdims=True)


def product(x, weights, part):
    rows = pl.ds(pl.multiple_of(part * x.shape[1], x.shape[1]), x.shape[1])
    return [jnp.dot(x, w[rows, :], preferred_element_type=jnp.float32) for w in weights]


def own_kernel(where, ha, hb, gain, wk, wv, wq, part, squares):
    squares[...] = squared(ha[...]) + squared(hb[...])
    tp = where[0]
    x = jnp.concatenate([gained(ha[...], gain[2 * tp]), gained(hb[...], gain[2 * tp + 1])], axis=1)
    start = 0
    for values in product(x, (wk, wv, wq), tp):
        part[:, start : start + values.shape[1]] = values
        start += values.shape[1]


def more_kernel(where, h, gain, wk, wv, wq, old, old_squares, part, squares):
    squares[...] = old_squares[...] + squared(h[...])
    start = 0
    part_in = 2 - 2 * where[0]
    for values in product(gained(h[...], gain[part_in]), (wk, wv, wq), part_in):
        cols = slice(start, start + values.shape[1])
        part[:, cols] = old[:, cols] + values
        start += values.shape[1]


def last_kernel(where, h, gain, wk, wv, wq, old, old_squares, cos, sin, kv_mine, q_mine, q_other, other):
    total = old_squares[...] + squared(h[...])
    factor = lax.rsqrt(total / (4 * h.shape[1]) + NORM_EPS)
    part_in = 3 - 2 * where[0]
    keys, values, queries = product(gained(h[...], gain[part_in]), (wk, wv, wq), part_in)
    width = 2 * HD
    keys = (old[:, :width] + keys) * factor
    values = (old[:, width : 2 * width] + values) * factor
    queries = (old[:, 2 * width :] + queries) * (factor * (1.0 / HD**0.5 * math.log2(math.e)))

    def columns(array, head):
        return array[:, head * HD : (head + 1) * HD]

    def sides(array, axis):
        return jnp.split(array.astype(jnp.bfloat16), 2, axis=axis)

    groups = []
    for group in range(2):
        key = sides(turn(columns(keys, group), cos[...], sin[...]), 0)
        value = sides(columns(values, group).T, 1)
        kv = [key[0], value[0], key[1], value[1]]
        q = []
        for head in range(GROUP):
            q += sides(turn(columns(queries, group * GROUP + head), cos[...], sin[...]).T, 1)
        groups.append((kv, q))

    def write(mine, others):
        for i in range(KV_TILES):
            kv_mine[i // 2, i % 2] = mine[0][i]
            other[i] = others[0][i]
        for i in range(Q_TILES):
            q_mine[i // 2, i % 2] = mine[1][i]
            q_other[i // 2, i % 2] = others[1][i]
            other[KV_TILES + i] = others[1][i]

    pl.when(where[1] == 0)(lambda: write(*groups))
    pl.when(where[1] == 1)(lambda: write(*groups[::-1]))


def project(kernel, where, ins, outs, time, name):
    return pl.pallas_call(
        kernel,
        in_specs=[smem()] + [vmem()] * len(ins),
        out_specs=[vmem()] * len(outs),
        out_shape=[jax.ShapeDtypeStruct(shape, dtype) for shape, dtype in outs],
        compiler_params=params(),
        cost_estimate=takes(time),
        name=name,
    )(where, *ins)


def project_own(where, ha, hb, gain, weights):
    rows, cols = ha.shape[0], sum(w.shape[1] for w in weights)
    outs = [((rows, cols), jnp.float32), ((rows, 1), jnp.float32)]
    return project(own_kernel, where, (ha, hb, gain, *weights), outs, 5, "project_own")


def project_more(where, h, gain, weights, partial):
    outs = [(array.shape, array.dtype) for array in partial]
    return project(more_kernel, where, (h, gain, *weights, *partial), outs, 2, "project_more")


def project_last(where, h, gain, weights, partial, cos, sin):
    q = (GROUP, 2, HD, HALF)
    shapes = [(2, 2, HALF, HD), q, q, (KV_TILES + Q_TILES, HALF, HD)]
    outs = [(shape, jnp.bfloat16) for shape in shapes]
    return project(last_kernel, where, (h, gain, *weights, *partial, cos, sin), outs, 2, "project_last")


ONES = 16


def attend_kernel(counts, diag, resume, finish, waits, *refs):
    flags, q, refs = refs[0], refs[1], refs[2:]
    kvs, refs = refs[: len(counts)], refs[len(counts) :]
    olds = refs[:3] if resume else ()
    refs = refs[len(olds) + waits :]
    parts = ()
    if finish:
        parts, refs = refs[:2], refs[2:]
    acc, den, top, klist, vlist = refs
    total = klist.shape[0]

    if resume:
        acc[...] = olds[0][...]
        den[...] = olds[1][...]
        top[...] = olds[2][...]
    else:
        acc[...] = jnp.zeros_like(acc)
        den[...] = jnp.zeros_like(den)
        top[...] = jnp.full_like(top, NEG_FILL)

    vlist[:, HD:, :] = jnp.ones((total, ONES, 2 * HALF), jnp.bfloat16)

    def put(place, kv, block, side):
        for core in range(2):
            span = slice(core * HALF, (core + 1) * HALF)
            klist[place, span, :] = kv[block, core, side, 0]
            vlist[place, :HD, span] = kv[block, core, side, 1]

    last = total - 2 if diag else total - 1
    front, back = jnp.int32(0), jnp.int32(last)
    start = 0
    for kv, count in zip(kvs, counts):
        for block in range(count):
            put(front, kv, block, 0)
            front = front + 1
            if diag and start + block == 0:
                continue
            early = flags[start + block]
            put(jnp.where(early == 1, back, front), kv, block, 1 - early)
            front = front + 1 - early
            back = back - early
        start += count
    n_late = front
    n_early = last - back

    def update(side, places, mask):
        keys = jnp.concatenate([klist[p] for p in places], axis=0)
        scores = []
        for head in range(GROUP):
            columns = jnp.concatenate([q[0, head, side], q[1, head, side]], axis=1)
            scores.append(jnp.dot(keys, columns, preferred_element_type=jnp.float32))
        values = jnp.concatenate([vlist[p] for p in places], axis=1)
        for head in range(GROUP):
            s = scores[head]
            if mask is not None:
                s = jnp.where(mask, s, NEG_FILL)
            old = top[side, head]
            new = jnp.maximum(old, jnp.max(s, axis=0, keepdims=True))
            weights = jnp.exp2(s - new[:1]).astype(jnp.bfloat16)
            prod = jnp.dot(values, weights, preferred_element_type=jnp.float32)
            keep = jnp.exp2(old - new)
            acc[side, head] = acc[side, head] * keep[:1] + prod[:HD]
            den[side, head] = den[side, head] * keep + prod[HD : HD + 8]
            top[side, head] = new

    if diag:
        core = flags[0]
        row = lax.broadcasted_iota(jnp.int32, (2 * HALF, 2 * HALF), 0)
        col = lax.broadcasted_iota(jnp.int32, (2 * HALF, 2 * HALF), 1)

        def own(side, carry):
            first = jnp.where(side == 0, core, 1 - core)
            key_pos = jnp.where(row < HALF, row + first * HALF, row - first * HALF)
            query_pos = jnp.where(col < HALF, col + first * HALF, col - first * HALF)
            put(total - 1, kvs[0], 0, side)
            update(side, (total - 1,), key_pos <= query_pos)
            return carry

        lax.fori_loop(0, 2, own, 0)

    pairs = n_late // 2
    early_pairs = n_early // 2
    def two(i, carry):
        late = i < pairs
        j = i - pairs
        one = jnp.where(late, 2 * i, last - 2 * j)
        other = jnp.where(late, 2 * i + 1, last - 2 * j - 1)
        update(jnp.where(late, 1, 0), (one, other), None)
        return carry

    lax.fori_loop(0, pairs + early_pairs, two, 0)
    odd_late = n_late - 2 * pairs
    odd_early = n_early - 2 * early_pairs

    def one(i, carry):
        late = i < odd_late
        update(jnp.where(late, 1, 0), (jnp.where(late, n_late - 1, last - n_early + 1),), None)
        return carry

    lax.fori_loop(0, odd_late + odd_early, one, 0)

    if finish:
        write_parts(acc, den, top, parts)


def write_parts(acc, den, top, parts):
    for side in range(2):
        for head in range(GROUP):
            denominator = den[side, head]
            some = denominator > 0.0
            safe = jnp.where(some, denominator, 1.0)
            inverse = jnp.where(some, 1.0 / safe, 0.0)
            value = (acc[side, head] * inverse[:1]).astype(jnp.bfloat16)
            level = jnp.where(some, top[side, head] + jnp.log2(safe), NEG_FILL)
            high = level.astype(jnp.bfloat16)
            low = (level - high.astype(jnp.float32)).astype(jnp.bfloat16)
            levels = jnp.concatenate([high, low], axis=0)
            for core in range(2):
                rows = slice(core * HALF, (core + 1) * HALF)
                parts[core][side, head, :HD] = value[:, rows]
                parts[core][side, head, HD:] = levels[:, rows]


ACC = (2, GROUP, HD, 2 * HALF)
ROWS = (2, GROUP, 8, 2 * HALF)
PART = (2, GROUP, HD + 16, HALF)


def attend(flags, q, kvs, state, diag=False, finish=False, after=(), time=None):
    counts = tuple(kv.shape[0] for kv in kvs)
    n = sum(counts)
    total = 2 * n
    olds = [] if state is None else list(state)
    states = (ACC, ROWS, ROWS)
    scratch = [
        pltpu.VMEM((total, 2 * HALF, HD), jnp.bfloat16),
        pltpu.VMEM((total, HD + ONES, 2 * HALF), jnp.bfloat16),
    ]
    if finish:
        shapes = [jax.ShapeDtypeStruct(PART, jnp.bfloat16)] * 2
        scratch = [pltpu.VMEM(shape, jnp.float32) for shape in states] + scratch
    else:
        shapes = [jax.ShapeDtypeStruct(shape, jnp.float32) for shape in states]
    return pl.pallas_call(
        functools.partial(attend_kernel, counts, diag, state is not None, finish, len(after)),
        in_specs=[smem()] + [vmem()] * (1 + len(kvs) + len(olds)) + [anywhere()] * len(after),
        out_specs=[vmem()] * len(shapes),
        out_shape=shapes,
        scratch_shapes=scratch,
        compiler_params=params(),
        cost_estimate=takes(1.15 * n if time is None else time),
        name="attend",
    )(flags, q, *kvs, *olds, *after)


def divide_kernel(waits, *refs):
    acc, den, top = refs[:3]
    write_parts(acc, den, top, refs[3 + waits :])


def divide(state, after):
    return pl.pallas_call(
        functools.partial(divide_kernel, len(after)),
        in_specs=[vmem()] * 3 + [anywhere()] * len(after),
        out_specs=[vmem()] * 2,
        out_shape=[jax.ShapeDtypeStruct(PART, jnp.bfloat16)] * 2,
        compiler_params=params(),
        cost_estimate=takes(0.7),
        name="divide",
    )(*state, *after)


def join_kernel(*refs):
    out = refs[-1]
    for i in range(out.shape[0]):
        out[i] = refs[i][0]


def join(blocks, after):
    return pl.pallas_call(
        join_kernel,
        in_specs=[vmem()] * len(blocks) + [anywhere()],
        out_specs=vmem(),
        out_shape=jax.ShapeDtypeStruct((len(blocks),) + blocks[0].shape[1:], jnp.bfloat16),
        compiler_params=params(),
        cost_estimate=takes(0.3),
        name="join",
    )(*blocks, after)


def merge_kernel(core, own, own_pair, sibling, sibling_pair, out):
    def level(part, side, head):
        return part[side, head, HD : HD + 8].astype(jnp.float32)[:1] + part[
            side, head, HD + 8 :
        ].astype(jnp.float32)[:1]

    for group, (one, two) in ((core[0], (own, own_pair)), (1 - core[0], (sibling, sibling_pair))):
        for side in range(2):
            for head in range(GROUP):
                mine, other = level(one, side, head), level(two, side, head)
                top = jnp.maximum(mine, other)
                first = jnp.exp2(mine - top)
                second = jnp.exp2(other - top)
                weight = 1.0 / (first + second)
                value = one[side, head, :HD].astype(jnp.float32) * (first * weight)
                value = value + two[side, head, :HD].astype(jnp.float32) * (second * weight)
                cols = pl.ds(pl.multiple_of((group * GROUP + head) * HD, HD), HD)
                out[side * HALF : (side + 1) * HALF, cols] = value.T.astype(jnp.bfloat16)


def merge(core, own, own_pair, sibling, sibling_pair):
    return pl.pallas_call(
        merge_kernel,
        in_specs=[smem()] + [vmem()] * 4,
        out_specs=vmem(),
        out_shape=jax.ShapeDtypeStruct((2 * HALF, 2 * GROUP * HD), jnp.bfloat16),
        compiler_params=params(),
        name="merge",
    )(core, own, own_pair, sibling, sibling_pair)


def rotations(ctx_index, rows):
    row = jnp.arange(rows, dtype=jnp.int32)
    half = rows // 2
    count = NY * NZ * NX * NK
    pos = jnp.where(row < half, ctx_index * half + row, (2 * count - 1 - ctx_index) * half + row - half)
    frequency = ROPE_BASE ** (-(jnp.arange(HD // 2, dtype=jnp.float32) * 2.0 / HD))
    angles = pos.astype(jnp.float32)[:, None] * frequency[None, :]
    cos, sin = jnp.cos(angles), jnp.sin(angles)
    return jnp.concatenate([cos, cos], axis=1), jnp.concatenate([-sin, sin], axis=1)


def chip_order(y, z, x):
    return (y * NZ + z) * NX + x


def shards(residual, shared_out, expert_out, routing, gate_score, norm_gain, w_query, w_key, w_value):
    rows, half_width = residual.shape
    ctx_index = lax.axis_index("ctx")
    tp_index = lax.axis_index("tp")
    y, z, x, k = split_index(ctx_index)
    cos, sin = rotations(ctx_index, rows)

    own_experts, sources, slots, _ = expert_out.shape
    returned = lax.all_to_all(relayout(expert_out), "ctx", split_axis=0, concat_axis=0, tiled=True)
    returned = returned.reshape(sources * own_experts * slots, half_width)
    hot = choose(routing, returned.shape[0])
    ha = pick(0, hot, gate_score, returned, residual, shared_out, hot)
    hb = pick(1, hot, gate_score, returned, residual, shared_out, ha)
    hidden = jnp.concatenate([ha, hb], axis=1)

    other_a, other_b = (lax.ppermute(h, "tp", [(0, 1), (1, 0)]) for h in (ha, hb))
    where = jnp.stack([tp_index, k])
    gain = norm_gain.reshape(4, 1, half_width // 2)
    weights = (w_key, w_value, w_query)
    partial = project_own(where, ha, hb, gain, weights)
    partial = project_more(where, other_a, gain, weights, partial)
    kv_mine, q_mine, q_other, to_other = project_last(where, other_b, gain, weights, partial, cos, sin)

    from_other = core_swap(to_other)
    block = jnp.stack([kv_mine, from_other[:KV_TILES].reshape(kv_mine.shape)])[None]
    q_own = jnp.stack([q_mine, from_other[KV_TILES:].reshape(q_mine.shape)])
    q_pair = jnp.stack([to_pair(q_mine), to_pair_other(q_other)])

    near = [first_axis(block, step) for step in (1, -1, 2)]
    own_state = attend(k.reshape(1), q_own, [block], None, diag=True, time=30)
    line = join([block] + near, own_state[2])
    ahead, behind = second_axis(line, 1), second_axis(line, -1)
    far = [ahead, behind, second_axis(ahead[:2], 1), second_axis(behind[2:], -1)]

    steps = jnp.array([0, 1, -1, 2], jnp.int32)

    def before(first, second, chip):
        by = jnp.where(k == 0, second, first)
        bx = jnp.where(k == 0, first, second)
        return (chip_order((y + by) % NY, z, (x + bx) % NX) < chip).astype(jnp.int32)

    zero = jnp.zeros((4,), jnp.int32)
    own_flags, pair_flags = (
        jnp.concatenate([before(steps, zero + step, chip_order(y, at, x)) for step in (0, 1, -1, 2)])
        for at in (z, 1 - z)
    )
    pair_state = attend(pair_flags[:4], q_pair, [line], None, time=7)
    pair_state = attend(pair_flags[4:12], q_pair, far[:2], pair_state)
    pair_same, pair_other = attend(pair_flags[12:], q_pair, far[2:], pair_state, finish=True)
    own_pair, sibling_pair = to_pair(pair_same), to_pair_other(pair_other)
    own_state = attend(own_flags[1:], q_own, near + far, own_state, after=(pair_same,))
    own_same, own_other = divide(own_state, (own_pair, sibling_pair))
    attended = merge(k.reshape(1), own_same, own_pair, core_swap(own_other), sibling_pair)
    return hidden, attended


def solution(mesh):
    return jax.shard_map(
        shards,
        mesh=mesh,
        in_specs=(
            P("ctx", "tp"),
            P("ctx", "tp"),
            P("ctx", None, None, "tp"),
            P("ctx", None),
            P("ctx", None),
            P(),
            P(None, "tp"),
            P(None, "tp"),
            P(None, "tp"),
        ),
        out_specs=(P("ctx", "tp"), P("ctx", "tp")),
        check_vma=False,
    )
```

```python
import functools
import math

import jax
import jax.numpy as jnp
from jax import lax
from jax.experimental import pallas as pl
from jax.experimental.pallas import tpu as pltpu
from jax.sharding import PartitionSpec as P

HD = 128
ROPE_BASE = 500000.0
NORM_EPS = 1e-05
NEG_FILL = -1e30
NY, NZ, NX, NK = 4, 2, 4, 2
GROUP = 5
HALF = 128
ALONE = 60
def split_index(c):
    return c // (NZ * NX * NK), (c // (NX * NK)) % NZ, (c // NK) % NX, c % NK


def join_index(y, z, x, k):
    return (((y % NY) * NZ + z % NZ) * NX + x % NX) * NK + k % NK


def permute(value, move):
    pairs = [(c, join_index(*move(*split_index(c)))) for c in range(NY * NZ * NX * NK)]
    return lax.ppermute(value, "ctx", pairs)


def core_swap(value):
    return permute(value, lambda y, z, x, k: (y, z, x, 1 - k))


def to_pair(value):
    return permute(value, lambda y, z, x, k: (y, 1 - z, x, k))


def to_pair_other(value):
    return permute(value, lambda y, z, x, k: (y, 1 - z, x, 1 - k))


def first_axis(value, step):
    return permute(
        value, lambda y, z, x, k: (y, z, x - step, k) if k == 0 else (y - step, z, x, k)
    )


def second_axis(value, step):
    return permute(
        value, lambda y, z, x, k: (y - step, z, x, k) if k == 0 else (y, z, x - step, k)
    )


def params(mib=24):
    return pltpu.CompilerParams(vmem_limit_bytes=mib * 1024 * 1024)


def takes(microseconds):
    return pl.CostEstimate(flops=int(microseconds * 1.15e9), bytes_accessed=0, transcendentals=0)


def vmem():
    return pl.BlockSpec(memory_space=pltpu.VMEM)


def anywhere():
    return pl.BlockSpec(memory_space=pl.ANY)


def hbm():
    return pl.BlockSpec(memory_space=pltpu.HBM)


def smem():
    return pl.BlockSpec(memory_space=pltpu.SMEM)


def choose_kernel(ids_col, ids_row, hot):
    rows = ids_col.shape[0]
    same = ids_col[...] == ids_row[...]
    row = lax.broadcasted_iota(jnp.int32, (rows, rows), 0)
    col = lax.broadcasted_iota(jnp.int32, (rows, rows), 1)
    slot = jnp.sum(jnp.where(same & (col < row), 1.0, 0.0), axis=1, keepdims=True)
    place = ids_col[...] * 4 + slot.astype(jnp.int32)
    lanes = lax.broadcasted_iota(jnp.int32, hot.shape, 1)
    hot[...] = jnp.where(lanes == place, 1.0, 0.0).astype(jnp.bfloat16)


def choose(ids, slots):
    rows = ids.shape[0]
    return pl.pallas_call(
        choose_kernel,
        in_specs=[vmem()] * 2,
        out_specs=vmem(),
        out_shape=jax.ShapeDtypeStruct((rows, slots), jnp.bfloat16),
        compiler_params=params(),
        cost_estimate=pl.CostEstimate(flops=2_000_000, bytes_accessed=600_000, transcendentals=0),
        name="choose",
    )(ids, ids.reshape(1, rows))


def relayout_kernel(experts, out, loaded, ready, arrive, leave):
    chunks, group = loaded.shape[0], loaded.shape[2]

    def load(i):
        return pltpu.make_async_copy(experts.at[:, pl.ds(i * group, group)], loaded.at[i], arrive.at[i])

    def store(i):
        return pltpu.make_async_copy(ready.at[i], out.at[pl.ds(i * group, group)], leave.at[i])

    for i in range(chunks):
        load(i).start()
    for i in range(chunks):
        load(i).wait()
        ready[i] = jnp.concatenate([loaded[i, e] for e in range(experts.shape[0])], axis=1)
        store(i).start()
    for i in range(chunks):
        store(i).wait()


def relayout(expert_out):
    experts, sources, slots, width = expert_out.shape
    chunks = 8
    group = sources // chunks
    return pl.pallas_call(
        relayout_kernel,
        in_specs=[anywhere()],
        out_specs=anywhere(),
        out_shape=jax.ShapeDtypeStruct((sources, experts * slots, width), jnp.bfloat16),
        scratch_shapes=[
            pltpu.VMEM((chunks, experts, group, slots, width), jnp.bfloat16),
            pltpu.VMEM((chunks, group, experts * slots, width), jnp.bfloat16),
            pltpu.SemaphoreType.DMA((chunks,)),
            pltpu.SemaphoreType.DMA((chunks,)),
        ],
        compiler_params=params(ALONE),
        name="relayout",
    )(expert_out)


def pick_kernel(first, hot, gate, returned, residual, shared, after, out, base, extra, done, arrive, leave):
    chunks, block, width = base.shape
    cols = slice(first, first + width)

    def loads(i):
        rows = pl.ds(i * block, block)
        return [
            pltpu.make_async_copy(residual.at[rows, cols], base.at[i], arrive.at[0, i]),
            pltpu.make_async_copy(shared.at[rows, cols], extra.at[i], arrive.at[1, i]),
        ]

    def store(i):
        return pltpu.make_async_copy(done.at[i], out.at[pl.ds(i * block, block)], leave.at[i])

    for i in range(chunks):
        for copy in loads(i):
            copy.start()
    for i in range(chunks):
        rows = slice(i * block, (i + 1) * block)
        picked = jnp.dot(hot[rows], returned[:, cols], preferred_element_type=jnp.float32)
        for copy in loads(i):
            copy.wait()
        total = base[i].astype(jnp.float32) + extra[i].astype(jnp.float32)
        done[i] = (total + gate[rows] * picked).astype(jnp.bfloat16)
        store(i).start()
    for i in range(chunks):
        store(i).wait()


def pick(part, hot, gate, returned, residual, shared, after):
    rows, width = residual.shape
    width = width // 2
    chunks = 2
    tile = pltpu.VMEM((chunks, rows // chunks, width), jnp.bfloat16)
    residual, shared = (pltpu.with_memory_space_constraint(a, pltpu.HBM) for a in (residual, shared))
    return pl.pallas_call(
        functools.partial(pick_kernel, part * width),
        in_specs=[vmem()] * 3 + [hbm()] * 2 + [anywhere()],
        out_specs=hbm(),
        out_shape=jax.ShapeDtypeStruct((rows, width), jnp.bfloat16),
        scratch_shapes=[
            tile,
            tile,
            tile,
            pltpu.SemaphoreType.DMA((2, chunks)),
            pltpu.SemaphoreType.DMA((chunks,)),
        ],
        compiler_params=params(10),
        cost_estimate=takes(2.5),
        name="pick",
    )(hot, gate, returned, residual, shared, after)


KV_TILES, Q_TILES = 4, 2 * GROUP


def turn(x, cos, sin):
    return x * cos + pltpu.roll(x, HD // 2, 1) * sin


def gained(h, gain):
    return (h.astype(jnp.float32) * gain.astype(jnp.float32)).astype(jnp.bfloat16)


def squared(h):
    wide = h.astype(jnp.float32)
    return jnp.sum(wide * wide, axis=1, keepdims=True)


def product(x, weights, part):
    rows = pl.ds(pl.multiple_of(part * x.shape[1], x.shape[1]), x.shape[1])
    return [jnp.dot(x, w[rows, :], preferred_element_type=jnp.float32) for w in weights]


def own_kernel(where, ha, hb, gain, wk, wv, wq, part, squares):
    squares[...] = squared(ha[...]) + squared(hb[...])
    tp = where[0]
    x = jnp.concatenate([gained(ha[...], gain[2 * tp]), gained(hb[...], gain[2 * tp + 1])], axis=1)
    start = 0
    for values in product(x, (wk, wv, wq), tp):
        part[:, start : start + values.shape[1]] = values
        start += values.shape[1]


def more_kernel(where, h, gain, wk, wv, wq, old, old_squares, part, squares):
    squares[...] = old_squares[...] + squared(h[...])
    start = 0
    part_in = 2 - 2 * where[0]
    for values in product(gained(h[...], gain[part_in]), (wk, wv, wq), part_in):
        cols = slice(start, start + values.shape[1])
        part[:, cols] = old[:, cols] + values
        start += values.shape[1]


def last_kernel(where, h, gain, wk, wv, wq, old, old_squares, cos, sin, kv_mine, q_mine, other):
    total = old_squares[...] + squared(h[...])
    factor = lax.rsqrt(total / (4 * h.shape[1]) + NORM_EPS)
    part_in = 3 - 2 * where[0]
    keys, values, queries = product(gained(h[...], gain[part_in]), (wk, wv, wq), part_in)
    width = 2 * HD
    keys = (old[:, :width] + keys) * factor
    values = (old[:, width : 2 * width] + values) * factor
    queries = (old[:, 2 * width :] + queries) * (factor * (1.0 / HD**0.5 * math.log2(math.e)))

    def columns(array, head):
        return array[:, head * HD : (head + 1) * HD]

    def sides(array, axis):
        return jnp.split(array.astype(jnp.bfloat16), 2, axis=axis)

    groups = []
    for group in range(2):
        key = sides(turn(columns(keys, group), cos[...], sin[...]), 0)
        value = sides(columns(values, group).T, 1)
        kv = [key[0], value[0], key[1], value[1]]
        q = []
        for head in range(GROUP):
            q += sides(turn(columns(queries, group * GROUP + head), cos[...], sin[...]).T, 1)
        groups.append((kv, q))

    def write(mine, others):
        for i in range(KV_TILES):
            kv_mine[i // 2, i % 2] = mine[0][i]
            other[i] = others[0][i]
        for i in range(Q_TILES):
            q_mine[i // 2, i % 2] = mine[1][i]
            other[KV_TILES + i] = others[1][i]

    pl.when(where[1] == 0)(lambda: write(*groups))
    pl.when(where[1] == 1)(lambda: write(*groups[::-1]))


def project(kernel, where, ins, outs, time, name):
    return pl.pallas_call(
        kernel,
        in_specs=[smem()] + [vmem()] * len(ins),
        out_specs=[vmem()] * len(outs),
        out_shape=[jax.ShapeDtypeStruct(shape, dtype) for shape, dtype in outs],
        compiler_params=params(),
        cost_estimate=takes(time),
        name=name,
    )(where, *ins)


def project_own(where, ha, hb, gain, weights):
    rows, cols = ha.shape[0], sum(w.shape[1] for w in weights)
    outs = [((rows, cols), jnp.float32), ((rows, 1), jnp.float32)]
    return project(own_kernel, where, (ha, hb, gain, *weights), outs, 5, "project_own")


def project_more(where, h, gain, weights, partial):
    outs = [(array.shape, array.dtype) for array in partial]
    return project(more_kernel, where, (h, gain, *weights, *partial), outs, 2, "project_more")


def project_last(where, h, gain, weights, partial, cos, sin):
    q = (GROUP, 2, HD, HALF)
    shapes = [(2, 2, HALF, HD), q, (KV_TILES + Q_TILES, HALF, HD)]
    outs = [(shape, jnp.bfloat16) for shape in shapes]
    return project(last_kernel, where, (h, gain, *weights, *partial, cos, sin), outs, 2, "project_last")


ONES = 16


def attend_kernel(counts, diag, resume, finish, waits, *refs):
    flags, q, refs = refs[0], refs[1], refs[2:]
    kvs, refs = refs[: len(counts)], refs[len(counts) :]
    olds = refs[:3] if resume else ()
    refs = refs[len(olds) + waits :]
    parts = ()
    if finish:
        parts, refs = refs[:2], refs[2:]
    acc, den, top, klist, vlist = refs
    total = klist.shape[0]

    if resume:
        acc[...] = olds[0][...]
        den[...] = olds[1][...]
        top[...] = olds[2][...]
    else:
        acc[...] = jnp.zeros_like(acc)
        den[...] = jnp.zeros_like(den)
        top[...] = jnp.full_like(top, NEG_FILL)

    vlist[:, HD:, :] = jnp.ones((total, ONES, 2 * HALF), jnp.bfloat16)

    def put(place, kv, block, side):
        for core in range(2):
            span = slice(core * HALF, (core + 1) * HALF)
            klist[place, span, :] = kv[block, core, side, 0]
            vlist[place, :HD, span] = kv[block, core, side, 1]

    last = total - 2 if diag else total - 1
    front, back = jnp.int32(0), jnp.int32(last)
    start = 0
    for kv, count in zip(kvs, counts):
        for block in range(count):
            put(front, kv, block, 0)
            front = front + 1
            if diag and start + block == 0:
                continue
            early = flags[start + block]
            put(jnp.where(early == 1, back, front), kv, block, 1 - early)
            front = front + 1 - early
            back = back - early
        start += count
    n_late = front
    n_early = last - back

    def update(side, places, mask):
        keys = jnp.concatenate([klist[p] for p in places], axis=0)
        scores = []
        for head in range(GROUP):
            columns = jnp.concatenate([q[0, head, side], q[1, head, side]], axis=1)
            scores.append(jnp.dot(keys, columns, preferred_element_type=jnp.float32))
        values = jnp.concatenate([vlist[p] for p in places], axis=1)
        for head in range(GROUP):
            s = scores[head]
            if mask is not None:
                s = jnp.where(mask, s, NEG_FILL)
            old = top[side, head]
            new = jnp.maximum(old, jnp.max(s, axis=0, keepdims=True))
            weights = jnp.exp2(s - new[:1]).astype(jnp.bfloat16)
            prod = jnp.dot(values, weights, preferred_element_type=jnp.float32)
            keep = jnp.exp2(old - new)
            acc[side, head] = acc[side, head] * keep[:1] + prod[:HD]
            den[side, head] = den[side, head] * keep + prod[HD : HD + 8]
            top[side, head] = new

    if diag:
        core = flags[0]
        row = lax.broadcasted_iota(jnp.int32, (2 * HALF, 2 * HALF), 0)
        col = lax.broadcasted_iota(jnp.int32, (2 * HALF, 2 * HALF), 1)

        def own(side, carry):
            first = jnp.where(side == 0, core, 1 - core)
            key_pos = jnp.where(row < HALF, row + first * HALF, row - first * HALF)
            query_pos = jnp.where(col < HALF, col + first * HALF, col - first * HALF)
            put(total - 1, kvs[0], 0, side)
            update(side, (total - 1,), key_pos <= query_pos)
            return carry

        lax.fori_loop(0, 2, own, 0)

    pairs = n_late // 2
    early_pairs = n_early // 2
    def two(i, carry):
        late = i < pairs
        j = i - pairs
        one = jnp.where(late, 2 * i, last - 2 * j)
        other = jnp.where(late, 2 * i + 1, last - 2 * j - 1)
        update(jnp.where(late, 1, 0), (one, other), None)
        return carry

    lax.fori_loop(0, pairs + early_pairs, two, 0)
    odd_late = n_late - 2 * pairs
    odd_early = n_early - 2 * early_pairs

    def one(i, carry):
        late = i < odd_late
        update(jnp.where(late, 1, 0), (jnp.where(late, n_late - 1, last - n_early + 1),), None)
        return carry

    lax.fori_loop(0, odd_late + odd_early, one, 0)

    if finish:
        write_parts(acc, den, top, parts)


def write_parts(acc, den, top, parts):
    for side in range(2):
        for head in range(GROUP):
            denominator = den[side, head]
            some = denominator > 0.0
            safe = jnp.where(some, denominator, 1.0)
            inverse = jnp.where(some, 1.0 / safe, 0.0)
            value = (acc[side, head] * inverse[:1]).astype(jnp.bfloat16)
            level = jnp.where(some, top[side, head] + jnp.log2(safe), NEG_FILL)
            high = level.astype(jnp.bfloat16)
            low = (level - high.astype(jnp.float32)).astype(jnp.bfloat16)
            levels = jnp.concatenate([high, low], axis=0)
            for core in range(2):
                rows = slice(core * HALF, (core + 1) * HALF)
                parts[core][side, head, :HD] = value[:, rows]
                parts[core][side, head, HD:] = levels[:, rows]


ACC = (2, GROUP, HD, 2 * HALF)
ROWS = (2, GROUP, 8, 2 * HALF)
PART = (2, GROUP, HD + 16, HALF)


def attend(flags, q, kvs, state, diag=False, finish=False, after=(), time=None):
    counts = tuple(kv.shape[0] for kv in kvs)
    n = sum(counts)
    total = 2 * n
    olds = [] if state is None else list(state)
    states = (ACC, ROWS, ROWS)
    scratch = [
        pltpu.VMEM((total, 2 * HALF, HD), jnp.bfloat16),
        pltpu.VMEM((total, HD + ONES, 2 * HALF), jnp.bfloat16),
    ]
    if finish:
        shapes = [jax.ShapeDtypeStruct(PART, jnp.bfloat16)] * 2
        scratch = [pltpu.VMEM(shape, jnp.float32) for shape in states] + scratch
    else:
        shapes = [jax.ShapeDtypeStruct(shape, jnp.float32) for shape in states]
    return pl.pallas_call(
        functools.partial(attend_kernel, counts, diag, state is not None, finish, len(after)),
        in_specs=[smem()] + [vmem()] * (1 + len(kvs) + len(olds)) + [anywhere()] * len(after),
        out_specs=[vmem()] * len(shapes),
        out_shape=shapes,
        scratch_shapes=scratch,
        compiler_params=params(),
        cost_estimate=takes(1.15 * n if time is None else time),
        name="attend",
    )(flags, q, *kvs, *olds, *after)


def divide_kernel(waits, *refs):
    acc, den, top = refs[:3]
    write_parts(acc, den, top, refs[3 + waits :])


def divide(state, after):
    return pl.pallas_call(
        functools.partial(divide_kernel, len(after)),
        in_specs=[vmem()] * 3 + [anywhere()] * len(after),
        out_specs=[vmem()] * 2,
        out_shape=[jax.ShapeDtypeStruct(PART, jnp.bfloat16)] * 2,
        compiler_params=params(),
        cost_estimate=takes(0.7),
        name="divide",
    )(*state, *after)


def join_kernel(*refs):
    out = refs[-1]
    for i in range(out.shape[0]):
        out[i] = refs[i][0]


def join(blocks, after):
    return pl.pallas_call(
        join_kernel,
        in_specs=[vmem()] * len(blocks) + [anywhere()],
        out_specs=vmem(),
        out_shape=jax.ShapeDtypeStruct((len(blocks),) + blocks[0].shape[1:], jnp.bfloat16),
        compiler_params=params(),
        cost_estimate=takes(0.3),
        name="join",
    )(*blocks, after)


def merge_kernel(core, own, own_pair, sibling, sibling_pair, out):
    def level(part, side, head):
        terms = part[side, head, HD:].astype(jnp.float32)
        return terms[:1] + terms[8:9]

    for group, (one, two) in ((core[0], (own, own_pair)), (1 - core[0], (sibling, sibling_pair))):
        for side in range(2):
            for head in range(GROUP):
                mine, other = level(one, side, head), level(two, side, head)
                top = jnp.maximum(mine, other)
                first = jnp.exp2(mine - top)
                second = jnp.exp2(other - top)
                weight = 1.0 / (first + second)
                value = one[side, head, :HD].astype(jnp.float32) * (first * weight)
                value = value + two[side, head, :HD].astype(jnp.float32) * (second * weight)
                cols = pl.ds(pl.multiple_of((group * GROUP + head) * HD, HD), HD)
                out[side * HALF : (side + 1) * HALF, cols] = value.T.astype(jnp.bfloat16)


def merge(core, own, own_pair, sibling, sibling_pair):
    return pl.pallas_call(
        merge_kernel,
        in_specs=[smem()] + [vmem()] * 4,
        out_specs=vmem(),
        out_shape=jax.ShapeDtypeStruct((2 * HALF, 2 * GROUP * HD), jnp.bfloat16),
        compiler_params=params(),
        name="merge",
    )(core, own, own_pair, sibling, sibling_pair)


def cut_kernel(ahead, behind, after, first, second):
    half = first.shape[0]
    first[...] = ahead[:half]
    second[...] = behind[half:]


def cut(ahead, behind, after):
    shape = (ahead.shape[0] // 2,) + ahead.shape[1:]
    return pl.pallas_call(
        cut_kernel,
        in_specs=[vmem()] * 2 + [anywhere()],
        out_specs=[vmem()] * 2,
        out_shape=[jax.ShapeDtypeStruct(shape, ahead.dtype)] * 2,
        compiler_params=params(8),
        cost_estimate=takes(0.3),
        name="cut",
    )(ahead, behind, after)


def rotations(ctx_index, rows):
    row = jnp.arange(rows, dtype=jnp.int32)
    half = rows // 2
    count = NY * NZ * NX * NK
    pos = jnp.where(row < half, ctx_index * half + row, (2 * count - 1 - ctx_index) * half + row - half)
    frequency = ROPE_BASE ** (-(jnp.arange(HD // 2, dtype=jnp.float32) * 2.0 / HD))
    angles = pos.astype(jnp.float32)[:, None] * frequency[None, :]
    cos, sin = jnp.cos(angles), jnp.sin(angles)
    return jnp.concatenate([cos, cos], axis=1), jnp.concatenate([-sin, sin], axis=1)


def chip_order(y, z, x):
    return (y * NZ + z) * NX + x


def shards(residual, shared_out, expert_out, routing, gate_score, norm_gain, w_query, w_key, w_value):
    rows, half_width = residual.shape
    ctx_index = lax.axis_index("ctx")
    tp_index = lax.axis_index("tp")
    y, z, x, k = split_index(ctx_index)
    cos, sin = rotations(ctx_index, rows)

    own_experts, sources, slots, _ = expert_out.shape
    returned = lax.all_to_all(relayout(expert_out), "ctx", split_axis=0, concat_axis=0, tiled=True)
    returned = returned.reshape(sources * own_experts * slots, half_width)
    hot = choose(routing, returned.shape[0])
    ha = pick(0, hot, gate_score, returned, residual, shared_out, hot)
    hb = pick(1, hot, gate_score, returned, residual, shared_out, ha)
    hidden = jnp.concatenate([ha, hb], axis=1)

    other_a, other_b = (lax.ppermute(h, "tp", [(0, 1), (1, 0)]) for h in (ha, hb))
    where = jnp.stack([tp_index, k])
    gain = norm_gain.reshape(4, 1, half_width // 2)
    weights = (w_key, w_value, w_query)
    partial = project_own(where, ha, hb, gain, weights)
    partial = project_more(where, other_a, gain, weights, partial)
    kv_mine, q_mine, to_other = project_last(where, other_b, gain, weights, partial, cos, sin)

    from_other = core_swap(to_other)
    block = jnp.stack([kv_mine, from_other[:KV_TILES].reshape(kv_mine.shape)])[None]
    q_own = jnp.stack([q_mine, from_other[KV_TILES:].reshape(q_mine.shape)])
    q_pair = to_pair(q_own)

    near = [first_axis(block, step) for step in (1, -1, 2)]
    own_state = attend(k.reshape(1), q_own, [block], None, diag=True, time=30)
    line = join([block] + near, own_state[2])
    steps = jnp.array([0, 1, -1, 2], jnp.int32)

    def before(first, second, chip):
        by = jnp.where(k == 0, second, first)
        bx = jnp.where(k == 0, first, second)
        return (chip_order((y + by) % NY, z, (x + bx) % NX) < chip).astype(jnp.int32)

    zero = jnp.zeros((4,), jnp.int32)
    own_flags, pair_flags = (
        jnp.concatenate([before(steps, zero + step, chip_order(y, at, x)) for step in (0, 1, -1, 2)])
        for at in (z, 1 - z)
    )
    ahead, behind = second_axis(line, 1), second_axis(line, -1)
    own_state = attend(own_flags[1:4], q_own, near, own_state, after=(line,))
    pair_state = attend(pair_flags[:4], q_pair, [line], None, after=(own_state[2],), time=7)
    far_ahead, far_behind = cut(ahead, behind, pair_state[2])
    farther = [second_axis(far_ahead, 1), second_axis(far_behind, -1)]
    pair_state = attend(pair_flags[4:12], q_pair, [ahead, behind], pair_state, after=(far_ahead,))
    pair_same, pair_other = attend(pair_flags[12:], q_pair, farther, pair_state, finish=True)
    own_pair, sibling_pair = to_pair(pair_same), to_pair_other(pair_other)
    own_state = attend(own_flags[4:], q_own, [ahead, behind] + farther, own_state, after=(pair_same,))
    own_same, own_other = divide(own_state, (own_pair, sibling_pair))
    attended = merge(k.reshape(1), own_same, own_pair, core_swap(own_other), sibling_pair)
    return hidden, attended


def solution(mesh):
    return jax.shard_map(
        shards,
        mesh=mesh,
        in_specs=(
            P("ctx", "tp"),
            P("ctx", "tp"),
            P("ctx", None, None, "tp"),
            P("ctx", None),
            P("ctx", None),
            P(),
            P(None, "tp"),
            P(None, "tp"),
            P(None, "tp"),
        ),
        out_specs=(P("ctx", "tp"), P("ctx", "tp")),
        check_vma=False,
    )
```

```python
import functools
import math

import jax
import jax.numpy as jnp
from jax import lax
from jax.experimental import pallas as pl
from jax.experimental.pallas import tpu as pltpu
from jax.sharding import PartitionSpec as P

HD = 128
ROPE_BASE = 500000.0
NORM_EPS = 1e-05
NEG_FILL = -1e30
NY, NZ, NX, NK = 4, 2, 4, 2
GROUP = 5
HALF = 128
ALONE = 60
def split_index(c):
    return c // (NZ * NX * NK), (c // (NX * NK)) % NZ, (c // NK) % NX, c % NK


def join_index(y, z, x, k):
    return (((y % NY) * NZ + z % NZ) * NX + x % NX) * NK + k % NK


def permute(value, move):
    pairs = [(c, join_index(*move(*split_index(c)))) for c in range(NY * NZ * NX * NK)]
    return lax.ppermute(value, "ctx", pairs)


def core_swap(value):
    return permute(value, lambda y, z, x, k: (y, z, x, 1 - k))


def to_pair(value):
    return permute(value, lambda y, z, x, k: (y, 1 - z, x, k))


def to_pair_other(value):
    return permute(value, lambda y, z, x, k: (y, 1 - z, x, 1 - k))


def first_axis(value, step):
    return permute(
        value, lambda y, z, x, k: (y, z, x - step, k) if k == 0 else (y - step, z, x, k)
    )


def second_axis(value, step):
    return permute(
        value, lambda y, z, x, k: (y - step, z, x, k) if k == 0 else (y, z, x - step, k)
    )


def params(mib=24):
    return pltpu.CompilerParams(vmem_limit_bytes=mib * 1024 * 1024)


def takes(microseconds):
    return pl.CostEstimate(flops=int(microseconds * 1.15e9), bytes_accessed=0, transcendentals=0)


def vmem():
    return pl.BlockSpec(memory_space=pltpu.VMEM)


def anywhere():
    return pl.BlockSpec(memory_space=pl.ANY)


def hbm():
    return pl.BlockSpec(memory_space=pltpu.HBM)


def smem():
    return pl.BlockSpec(memory_space=pltpu.SMEM)


def choose_kernel(ids_col, ids_row, hot):
    rows = ids_col.shape[0]
    same = ids_col[...] == ids_row[...]
    row = lax.broadcasted_iota(jnp.int32, (rows, rows), 0)
    col = lax.broadcasted_iota(jnp.int32, (rows, rows), 1)
    slot = jnp.sum(jnp.where(same & (col < row), 1.0, 0.0), axis=1, keepdims=True)
    place = ids_col[...] * 4 + slot.astype(jnp.int32)
    lanes = lax.broadcasted_iota(jnp.int32, hot.shape, 1)
    hot[...] = jnp.where(lanes == place, 1.0, 0.0).astype(jnp.bfloat16)


def choose(ids, slots):
    rows = ids.shape[0]
    return pl.pallas_call(
        choose_kernel,
        in_specs=[vmem()] * 2,
        out_specs=vmem(),
        out_shape=jax.ShapeDtypeStruct((rows, slots), jnp.bfloat16),
        compiler_params=params(),
        cost_estimate=pl.CostEstimate(flops=2_000_000, bytes_accessed=600_000, transcendentals=0),
        name="choose",
    )(ids, ids.reshape(1, rows))


def relayout_kernel(experts, out, loaded, ready, arrive, leave):
    chunks, group = loaded.shape[0], loaded.shape[2]

    def load(i):
        return pltpu.make_async_copy(experts.at[:, pl.ds(i * group, group)], loaded.at[i], arrive.at[i])

    def store(i):
        return pltpu.make_async_copy(ready.at[i], out.at[pl.ds(i * group, group)], leave.at[i])

    for i in range(chunks):
        load(i).start()
    for i in range(chunks):
        load(i).wait()
        ready[i] = jnp.concatenate([loaded[i, e] for e in range(experts.shape[0])], axis=1)
        store(i).start()
    for i in range(chunks):
        store(i).wait()


def relayout(expert_out):
    experts, sources, slots, width = expert_out.shape
    chunks = 8
    group = sources // chunks
    return pl.pallas_call(
        relayout_kernel,
        in_specs=[anywhere()],
        out_specs=anywhere(),
        out_shape=jax.ShapeDtypeStruct((sources, experts * slots, width), jnp.bfloat16),
        scratch_shapes=[
            pltpu.VMEM((chunks, experts, group, slots, width), jnp.bfloat16),
            pltpu.VMEM((chunks, group, experts * slots, width), jnp.bfloat16),
            pltpu.SemaphoreType.DMA((chunks,)),
            pltpu.SemaphoreType.DMA((chunks,)),
        ],
        compiler_params=params(ALONE),
        name="relayout",
    )(expert_out)


def pick_kernel(first, hot, gate, returned, residual, shared, before, *refs):
    hidden = refs[0]
    out, base, extra, done, arrive, leave = refs[-6:]
    chunks, block, width = base.shape
    cols = slice(first, first + width)

    def loads(i):
        rows = pl.ds(i * block, block)
        return [
            pltpu.make_async_copy(residual.at[rows, cols], base.at[i], arrive.at[0, i]),
            pltpu.make_async_copy(shared.at[rows, cols], extra.at[i], arrive.at[1, i]),
        ]

    def stores(i):
        rows = pl.ds(i * block, block)
        copies = [pltpu.make_async_copy(done.at[i], out.at[rows], leave.at[0, i])]
        if first > 0:
            copies.append(pltpu.make_async_copy(done.at[i], hidden.at[rows, cols], leave.at[1, i]))
            copies.append(pltpu.make_async_copy(before.at[rows], hidden.at[rows, :first], leave.at[2, i]))
        return copies

    for i in range(chunks):
        for copy in loads(i):
            copy.start()
    for i in range(chunks):
        rows = slice(i * block, (i + 1) * block)
        picked = jnp.dot(hot[rows], returned[:, cols], preferred_element_type=jnp.float32)
        for copy in loads(i):
            copy.wait()
        total = base[i].astype(jnp.float32) + extra[i].astype(jnp.float32)
        done[i] = (total + gate[rows] * picked).astype(jnp.bfloat16)
        for copy in stores(i):
            copy.start()
    for i in range(chunks):
        for copy in stores(i):
            copy.wait()


def pick(part, hot, gate, returned, residual, shared, before):
    rows, width = residual.shape
    width = width // 2
    chunks = 2
    tile = pltpu.VMEM((chunks, rows // chunks, width), jnp.bfloat16)
    residual, shared = (pltpu.with_memory_space_constraint(a, pltpu.HBM) for a in (residual, shared))
    return pl.pallas_call(
        functools.partial(pick_kernel, part * width),
        in_specs=[vmem()] * 3 + [hbm()] * 2 + [anywhere()],
        out_specs=[hbm()] * (part + 1),
        out_shape=[
            jax.ShapeDtypeStruct((rows, columns), jnp.bfloat16)
            for columns in ((2 * width, width) if part else (width,))
        ],
        scratch_shapes=[
            tile,
            tile,
            tile,
            pltpu.SemaphoreType.DMA((2, chunks)),
            pltpu.SemaphoreType.DMA((3, chunks)),
        ],
        compiler_params=params(10),
        cost_estimate=takes(2.5),
        name="pick",
    )(hot, gate, returned, residual, shared, before)


KV_TILES, Q_TILES = 4, 2 * GROUP


def turn(x, cos, sin):
    return x * cos + pltpu.roll(x, HD // 2, 1) * sin


def gained(h, gain):
    return (h.astype(jnp.float32) * gain.astype(jnp.float32)).astype(jnp.bfloat16)


def squared(h):
    wide = h.astype(jnp.float32)
    return jnp.sum(wide * wide, axis=1, keepdims=True)


def product(x, weights, part):
    rows = pl.ds(pl.multiple_of(part * x.shape[1], x.shape[1]), x.shape[1])
    return [jnp.dot(x, w[rows, :], preferred_element_type=jnp.float32) for w in weights]


def own_kernel(where, ha, hb, gain, wk, wv, wq, part, squares):
    squares[...] = squared(ha[...]) + squared(hb[...])
    tp = where[0]
    x = jnp.concatenate([gained(ha[...], gain[2 * tp]), gained(hb[...], gain[2 * tp + 1])], axis=1)
    start = 0
    for values in product(x, (wk, wv, wq), tp):
        part[:, start : start + values.shape[1]] = values
        start += values.shape[1]


def more_kernel(where, h, gain, wk, wv, wq, old, old_squares, part, squares):
    squares[...] = old_squares[...] + squared(h[...])
    start = 0
    part_in = 2 - 2 * where[0]
    for values in product(gained(h[...], gain[part_in]), (wk, wv, wq), part_in):
        cols = slice(start, start + values.shape[1])
        part[:, cols] = old[:, cols] + values
        start += values.shape[1]


def last_kernel(where, h, gain, wk, wv, wq, old, old_squares, cos, sin, kv_mine, q_mine, other):
    total = old_squares[...] + squared(h[...])
    factor = lax.rsqrt(total / (4 * h.shape[1]) + NORM_EPS)
    part_in = 3 - 2 * where[0]
    keys, values, queries = product(gained(h[...], gain[part_in]), (wk, wv, wq), part_in)
    width = 2 * HD
    keys = (old[:, :width] + keys) * factor
    values = (old[:, width : 2 * width] + values) * factor
    queries = (old[:, 2 * width :] + queries) * (factor * (1.0 / HD**0.5 * math.log2(math.e)))

    def columns(array, head):
        return array[:, head * HD : (head + 1) * HD]

    def sides(array, axis):
        return jnp.split(array.astype(jnp.bfloat16), 2, axis=axis)

    groups = []
    for group in range(2):
        key = sides(turn(columns(keys, group), cos[...], sin[...]), 0)
        value = sides(columns(values, group).T, 1)
        kv = [key[0], value[0], key[1], value[1]]
        q = []
        for head in range(GROUP):
            q += sides(turn(columns(queries, group * GROUP + head), cos[...], sin[...]).T, 1)
        groups.append((kv, q))

    def write(mine, others):
        for i in range(KV_TILES):
            kv_mine[i // 2, i % 2] = mine[0][i]
            other[i] = others[0][i]
        for i in range(Q_TILES):
            q_mine[i // 2, i % 2] = mine[1][i]
            other[KV_TILES + i] = others[1][i]

    pl.when(where[1] == 0)(lambda: write(*groups))
    pl.when(where[1] == 1)(lambda: write(*groups[::-1]))


def project(kernel, where, ins, outs, time, name):
    return pl.pallas_call(
        kernel,
        in_specs=[smem()] + [vmem()] * len(ins),
        out_specs=[vmem()] * len(outs),
        out_shape=[jax.ShapeDtypeStruct(shape, dtype) for shape, dtype in outs],
        compiler_params=params(),
        cost_estimate=takes(time),
        name=name,
    )(where, *ins)


def project_own(where, ha, hb, gain, weights):
    rows, cols = ha.shape[0], sum(w.shape[1] for w in weights)
    outs = [((rows, cols), jnp.float32), ((rows, 1), jnp.float32)]
    return project(own_kernel, where, (ha, hb, gain, *weights), outs, 5, "project_own")


def project_more(where, h, gain, weights, partial):
    outs = [(array.shape, array.dtype) for array in partial]
    return project(more_kernel, where, (h, gain, *weights, *partial), outs, 2, "project_more")


def project_last(where, h, gain, weights, partial, cos, sin):
    q = (GROUP, 2, HD, HALF)
    shapes = [(2, 2, HALF, HD), q, (KV_TILES + Q_TILES, HALF, HD)]
    outs = [(shape, jnp.bfloat16) for shape in shapes]
    return project(last_kernel, where, (h, gain, *weights, *partial, cos, sin), outs, 2, "project_last")


ONES = 16


def attend_kernel(counts, diag, resume, finish, waits, *refs):
    flags, q, refs = refs[0], refs[1], refs[2:]
    kvs, refs = refs[: len(counts)], refs[len(counts) :]
    olds = refs[:3] if resume else ()
    refs = refs[len(olds) + waits :]
    parts = ()
    if finish:
        parts, refs = refs[:2], refs[2:]
    acc, den, top, klist, vlist = refs
    total = klist.shape[0]

    if resume:
        acc[...] = olds[0][...]
        den[...] = olds[1][...]
        top[...] = olds[2][...]
    else:
        acc[...] = jnp.zeros_like(acc)
        den[...] = jnp.zeros_like(den)
        top[...] = jnp.full_like(top, NEG_FILL)

    vlist[:, HD:, :] = jnp.ones((total, ONES, 2 * HALF), jnp.bfloat16)

    def put(place, kv, block, side):
        for core in range(2):
            span = slice(core * HALF, (core + 1) * HALF)
            klist[place, span, :] = kv[block, core, side, 0]
            vlist[place, :HD, span] = kv[block, core, side, 1]

    last = total - 2 if diag else total - 1
    front, back = jnp.int32(0), jnp.int32(last)
    start = 0
    for kv, count in zip(kvs, counts):
        for block in range(count):
            put(front, kv, block, 0)
            front = front + 1
            if diag and start + block == 0:
                continue
            early = flags[start + block]
            put(jnp.where(early == 1, back, front), kv, block, 1 - early)
            front = front + 1 - early
            back = back - early
        start += count
    n_late = front
    n_early = last - back

    def update(side, places, mask):
        keys = jnp.concatenate([klist[p] for p in places], axis=0)
        scores = []
        for head in range(GROUP):
            columns = jnp.concatenate([q[0, head, side], q[1, head, side]], axis=1)
            scores.append(jnp.dot(keys, columns, preferred_element_type=jnp.float32))
        values = jnp.concatenate([vlist[p] for p in places], axis=1)
        for head in range(GROUP):
            s = scores[head]
            if mask is not None:
                s = jnp.where(mask, s, NEG_FILL)
            old = top[side, head]
            new = jnp.maximum(old, jnp.max(s, axis=0, keepdims=True))
            weights = jnp.exp2(s - new[:1]).astype(jnp.bfloat16)
            prod = jnp.dot(values, weights, preferred_element_type=jnp.float32)
            keep = jnp.exp2(old - new)
            acc[side, head] = acc[side, head] * keep[:1] + prod[:HD]
            den[side, head] = den[side, head] * keep + prod[HD : HD + 8]
            top[side, head] = new

    if diag:
        core = flags[0]
        row = lax.broadcasted_iota(jnp.int32, (2 * HALF, 2 * HALF), 0)
        col = lax.broadcasted_iota(jnp.int32, (2 * HALF, 2 * HALF), 1)

        def own(side, carry):
            first = jnp.where(side == 0, core, 1 - core)
            key_pos = jnp.where(row < HALF, row + first * HALF, row - first * HALF)
            query_pos = jnp.where(col < HALF, col + first * HALF, col - first * HALF)
            put(total - 1, kvs[0], 0, side)
            update(side, (total - 1,), key_pos <= query_pos)
            return carry

        lax.fori_loop(0, 2, own, 0)

    pairs = n_late // 2
    early_pairs = n_early // 2
    def two(i, carry):
        late = i < pairs
        j = i - pairs
        one = jnp.where(late, 2 * i, last - 2 * j)
        other = jnp.where(late, 2 * i + 1, last - 2 * j - 1)
        update(jnp.where(late, 1, 0), (one, other), None)
        return carry

    lax.fori_loop(0, pairs + early_pairs, two, 0)
    odd_late = n_late - 2 * pairs
    odd_early = n_early - 2 * early_pairs

    def one(i, carry):
        late = i < odd_late
        update(jnp.where(late, 1, 0), (jnp.where(late, n_late - 1, last - n_early + 1),), None)
        return carry

    lax.fori_loop(0, odd_late + odd_early, one, 0)

    if finish:
        write_parts(acc, den, top, parts)


def side_of(part, side):
    return part[side] if isinstance(part, tuple) else part.at[side]


def write_parts(acc, den, top, parts):
    for side in range(2):
        targets = [side_of(part, side) for part in parts]
        highs, lows = [], []
        for head in range(GROUP):
            denominator = den[side, head]
            some = denominator > 0.0
            safe = jnp.where(some, denominator, 1.0)
            inverse = jnp.where(some, 1.0 / safe, 0.0)
            value = (acc[side, head] * inverse[:1]).astype(jnp.bfloat16)
            level = jnp.where(some, top[side, head] + jnp.log2(safe), NEG_FILL)[:1]
            high = level.astype(jnp.bfloat16).astype(jnp.float32)
            highs.append(high)
            lows.append(level - high)
            for core, target in enumerate(targets):
                target[head * HD : (head + 1) * HD] = value[:, core * HALF : (core + 1) * HALF]
        filler = jnp.zeros((LOGS - 2 * GROUP, 2 * HALF), jnp.float32)
        levels = jnp.concatenate(highs + lows + [filler], axis=0).astype(jnp.bfloat16)
        for core, target in enumerate(targets):
            target[GROUP * HD :] = levels[:, core * HALF : (core + 1) * HALF]


ACC = (2, GROUP, HD, 2 * HALF)
ROWS = (2, GROUP, 8, 2 * HALF)
LOGS = 16
PART = (2, GROUP * HD + LOGS, HALF)


def attend(flags, q, kvs, state, diag=False, finish=False, after=(), time=None):
    counts = tuple(kv.shape[0] for kv in kvs)
    n = sum(counts)
    total = 2 * n
    olds = [] if state is None else list(state)
    states = (ACC, ROWS, ROWS)
    scratch = [
        pltpu.VMEM((total, 2 * HALF, HD), jnp.bfloat16),
        pltpu.VMEM((total, HD + ONES, 2 * HALF), jnp.bfloat16),
    ]
    if finish:
        shapes = [jax.ShapeDtypeStruct(PART, jnp.bfloat16)] * 2
        scratch = [pltpu.VMEM(shape, jnp.float32) for shape in states] + scratch
    else:
        shapes = [jax.ShapeDtypeStruct(shape, jnp.float32) for shape in states]
    return pl.pallas_call(
        functools.partial(attend_kernel, counts, diag, state is not None, finish, len(after)),
        in_specs=[smem()] + [vmem()] * (1 + len(kvs) + len(olds)) + [anywhere()] * len(after),
        out_specs=[vmem()] * len(shapes),
        out_shape=shapes,
        scratch_shapes=scratch,
        compiler_params=params(),
        cost_estimate=takes(1.15 * n if time is None else time),
        name="attend",
    )(flags, q, *kvs, *olds, *after)


def divide_kernel(acc, den, top, after, same, other_early, other_late):
    write_parts(acc, den, top, (same, (other_early, other_late)))


def divide(state, after):
    shapes = (PART, PART[1:], PART[1:])
    return pl.pallas_call(
        divide_kernel,
        in_specs=[vmem()] * 3 + [anywhere()],
        out_specs=[vmem()] * 3,
        out_shape=[jax.ShapeDtypeStruct(shape, jnp.bfloat16) for shape in shapes],
        compiler_params=params(),
        cost_estimate=takes(0.7),
        name="divide",
    )(*state, after)


def join_kernel(*refs):
    out = refs[-1]
    for i in range(out.shape[0]):
        out[i] = refs[i][0]


def join(blocks, after):
    return pl.pallas_call(
        join_kernel,
        in_specs=[vmem()] * len(blocks) + [anywhere()],
        out_specs=vmem(),
        out_shape=jax.ShapeDtypeStruct((len(blocks),) + blocks[0].shape[1:], jnp.bfloat16),
        compiler_params=params(),
        cost_estimate=takes(0.3),
        name="join",
    )(*blocks, after)


def merge_kernel(core, own, own_pair, sibling_early, sibling_late, sibling_pair, out):
    def read(part, side):
        terms = side_of(part, side)[GROUP * HD :].astype(jnp.float32)
        values = side_of(part, side)[: GROUP * HD].astype(jnp.float32)
        return terms[:GROUP] + terms[GROUP : 2 * GROUP], values

    sibling = (sibling_early, sibling_late)
    for group, (one, two) in ((core[0], (own, own_pair)), (1 - core[0], (sibling, sibling_pair))):
        for side in range(2):
            mine, value = read(one, side)
            other, other_value = read(two, side)
            high = jnp.maximum(mine, other)
            first = jnp.exp2(mine - high)
            second = jnp.exp2(other - high)
            weight = 1.0 / (first + second)
            first, second = first * weight, second * weight
            for head in range(GROUP):
                rows = slice(head * HD, (head + 1) * HD)
                mixed = value[rows] * first[head : head + 1] + other_value[rows] * second[head : head + 1]
                cols = pl.ds(pl.multiple_of((group * GROUP + head) * HD, HD), HD)
                out[side * HALF : (side + 1) * HALF, cols] = mixed.T.astype(jnp.bfloat16)


def merge(core, own, own_pair, sibling_early, sibling_late, sibling_pair):
    return pl.pallas_call(
        merge_kernel,
        in_specs=[smem()] + [vmem()] * 5,
        out_specs=vmem(),
        out_shape=jax.ShapeDtypeStruct((2 * HALF, 2 * GROUP * HD), jnp.bfloat16),
        compiler_params=params(),
        name="merge",
    )(core, own, own_pair, sibling_early, sibling_late, sibling_pair)


def cut_kernel(ahead, behind, after, first, second):
    half = first.shape[0]
    first[...] = ahead[:half]
    second[...] = behind[half:]


def cut(ahead, behind, after):
    shape = (ahead.shape[0] // 2,) + ahead.shape[1:]
    return pl.pallas_call(
        cut_kernel,
        in_specs=[vmem()] * 2 + [anywhere()],
        out_specs=[vmem()] * 2,
        out_shape=[jax.ShapeDtypeStruct(shape, ahead.dtype)] * 2,
        compiler_params=params(8),
        cost_estimate=takes(0.3),
        name="cut",
    )(ahead, behind, after)


def rotations(ctx_index, rows):
    row = jnp.arange(rows, dtype=jnp.int32)
    half = rows // 2
    count = NY * NZ * NX * NK
    pos = jnp.where(row < half, ctx_index * half + row, (2 * count - 1 - ctx_index) * half + row - half)
    frequency = ROPE_BASE ** (-(jnp.arange(HD // 2, dtype=jnp.float32) * 2.0 / HD))
    angles = pos.astype(jnp.float32)[:, None] * frequency[None, :]
    cos, sin = jnp.cos(angles), jnp.sin(angles)
    return jnp.concatenate([cos, cos], axis=1), jnp.concatenate([-sin, sin], axis=1)


def chip_order(y, z, x):
    return (y * NZ + z) * NX + x


def shards(residual, shared_out, expert_out, routing, gate_score, norm_gain, w_query, w_key, w_value):
    rows, half_width = residual.shape
    ctx_index = lax.axis_index("ctx")
    tp_index = lax.axis_index("tp")
    y, z, x, k = split_index(ctx_index)
    cos, sin = rotations(ctx_index, rows)

    own_experts, sources, slots, _ = expert_out.shape
    returned = lax.all_to_all(relayout(expert_out), "ctx", split_axis=0, concat_axis=0, tiled=True)
    returned = returned.reshape(sources * own_experts * slots, half_width)
    hot = choose(routing, returned.shape[0])
    (ha,) = pick(0, hot, gate_score, returned, residual, shared_out, hot)
    hidden, hb = pick(1, hot, gate_score, returned, residual, shared_out, ha)

    other_a, other_b = (lax.ppermute(h, "tp", [(0, 1), (1, 0)]) for h in (ha, hb))
    where = jnp.stack([tp_index, k])
    gain = norm_gain.reshape(4, 1, half_width // 2)
    weights = (w_key, w_value, w_query)
    partial = project_own(where, ha, hb, gain, weights)
    partial = project_more(where, other_a, gain, weights, partial)
    kv_mine, q_mine, to_other = project_last(where, other_b, gain, weights, partial, cos, sin)

    from_other = core_swap(to_other)
    block = jnp.stack([kv_mine, from_other[:KV_TILES].reshape(kv_mine.shape)])[None]
    q_own = jnp.stack([q_mine, from_other[KV_TILES:].reshape(q_mine.shape)])
    q_pair = to_pair(q_own)

    near = [first_axis(block, step) for step in (1, -1, 2)]
    own_state = attend(k.reshape(1), q_own, [block], None, diag=True, time=30)
    line = join([block] + near, own_state[2])
    steps = jnp.array([0, 1, -1, 2], jnp.int32)

    def before(first, second, chip):
        by = jnp.where(k == 0, second, first)
        bx = jnp.where(k == 0, first, second)
        return (chip_order((y + by) % NY, z, (x + bx) % NX) < chip).astype(jnp.int32)

    zero = jnp.zeros((4,), jnp.int32)
    own_flags, pair_flags = (
        jnp.concatenate([before(steps, zero + step, chip_order(y, at, x)) for step in (0, 1, -1, 2)])
        for at in (z, 1 - z)
    )
    ahead, behind = second_axis(line, 1), second_axis(line, -1)
    own_state = attend(own_flags[1:4], q_own, near, own_state, after=(line,))
    pair_state = attend(pair_flags[:4], q_pair, [line], None, after=(own_state[2],), time=7)
    far_ahead, far_behind = cut(ahead, behind, pair_state[2])
    farther = [second_axis(far_ahead, 1), second_axis(far_behind, -1)]
    pair_state = attend(pair_flags[4:12], q_pair, [ahead, behind], pair_state, after=(far_ahead,))
    pair_same, pair_other = attend(pair_flags[12:], q_pair, farther, pair_state, finish=True)
    own_pair, sibling_pair = to_pair(pair_same), to_pair_other(pair_other)
    own_state = attend(own_flags[4:], q_own, [ahead, behind] + farther, own_state, after=(pair_same,))
    own_same, *own_other = divide(own_state, sibling_pair)
    siblings = [core_swap(part) for part in own_other]
    attended = merge(k.reshape(1), own_same, own_pair, *siblings, sibling_pair)
    return hidden, attended


def solution(mesh):
    return jax.shard_map(
        shards,
        mesh=mesh,
        in_specs=(
            P("ctx", "tp"),
            P("ctx", "tp"),
            P("ctx", None, None, "tp"),
            P("ctx", None),
            P("ctx", None),
            P(),
            P(None, "tp"),
            P(None, "tp"),
            P(None, "tp"),
        ),
        out_specs=(P("ctx", "tp"), P("ctx", "tp")),
        check_vma=False,
    )
```

```python
import functools
import math

import jax
import jax.numpy as jnp
from jax import lax
from jax.experimental import pallas as pl
from jax.experimental.pallas import tpu as pltpu
from jax.sharding import PartitionSpec as P

HD = 128
ROPE_BASE = 500000.0
NORM_EPS = 1e-05
NEG_FILL = -1e30
NY, NZ, NX, NK = 4, 2, 4, 2
GROUP = 5
HALF = 128
ALONE = 60
def split_index(c):
    return c // (NZ * NX * NK), (c // (NX * NK)) % NZ, (c // NK) % NX, c % NK


def join_index(y, z, x, k):
    return (((y % NY) * NZ + z % NZ) * NX + x % NX) * NK + k % NK


def permute(value, move):
    pairs = [(c, join_index(*move(*split_index(c)))) for c in range(NY * NZ * NX * NK)]
    return lax.ppermute(value, "ctx", pairs)


def core_swap(value):
    return permute(value, lambda y, z, x, k: (y, z, x, 1 - k))


def to_pair(value):
    return permute(value, lambda y, z, x, k: (y, 1 - z, x, k))


def to_pair_other(value):
    return permute(value, lambda y, z, x, k: (y, 1 - z, x, 1 - k))


def first_axis(value, step):
    return permute(
        value, lambda y, z, x, k: (y, z, x - step, k) if k == 0 else (y - step, z, x, k)
    )


def second_axis(value, step):
    return permute(
        value, lambda y, z, x, k: (y - step, z, x, k) if k == 0 else (y, z, x - step, k)
    )


def params(mib=24):
    return pltpu.CompilerParams(vmem_limit_bytes=mib * 1024 * 1024)


def takes(microseconds):
    return pl.CostEstimate(flops=int(microseconds * 1.15e9), bytes_accessed=0, transcendentals=0)


def vmem():
    return pl.BlockSpec(memory_space=pltpu.VMEM)


def anywhere():
    return pl.BlockSpec(memory_space=pl.ANY)


def hbm():
    return pl.BlockSpec(memory_space=pltpu.HBM)


def smem():
    return pl.BlockSpec(memory_space=pltpu.SMEM)


def choose_kernel(ids_col, ids_row, hot):
    rows = ids_col.shape[0]
    same = ids_col[...] == ids_row[...]
    row = lax.broadcasted_iota(jnp.int32, (rows, rows), 0)
    col = lax.broadcasted_iota(jnp.int32, (rows, rows), 1)
    slot = jnp.sum(jnp.where(same & (col < row), 1.0, 0.0), axis=1, keepdims=True)
    place = ids_col[...] * 4 + slot.astype(jnp.int32)
    lanes = lax.broadcasted_iota(jnp.int32, hot.shape, 1)
    hot[...] = jnp.where(lanes == place, 1.0, 0.0).astype(jnp.bfloat16)


def choose(ids, slots):
    rows = ids.shape[0]
    return pl.pallas_call(
        choose_kernel,
        in_specs=[vmem()] * 2,
        out_specs=vmem(),
        out_shape=jax.ShapeDtypeStruct((rows, slots), jnp.bfloat16),
        compiler_params=params(),
        cost_estimate=pl.CostEstimate(flops=2_000_000, bytes_accessed=600_000, transcendentals=0),
        name="choose",
    )(ids, ids.reshape(1, rows))


def relayout_kernel(experts, out, loaded, ready, arrive, leave):
    chunks, group = loaded.shape[0], loaded.shape[2]

    def load(i):
        return pltpu.make_async_copy(experts.at[:, pl.ds(i * group, group)], loaded.at[i], arrive.at[i])

    def store(i):
        return pltpu.make_async_copy(ready.at[i], out.at[pl.ds(i * group, group)], leave.at[i])

    for i in range(chunks):
        load(i).start()
    for i in range(chunks):
        load(i).wait()
        ready[i] = jnp.concatenate([loaded[i, e] for e in range(experts.shape[0])], axis=1)
        store(i).start()
    for i in range(chunks):
        store(i).wait()


def relayout(expert_out):
    experts, sources, slots, width = expert_out.shape
    chunks = 8
    group = sources // chunks
    return pl.pallas_call(
        relayout_kernel,
        in_specs=[anywhere()],
        out_specs=anywhere(),
        out_shape=jax.ShapeDtypeStruct((sources, experts * slots, width), jnp.bfloat16),
        scratch_shapes=[
            pltpu.VMEM((chunks, experts, group, slots, width), jnp.bfloat16),
            pltpu.VMEM((chunks, group, experts * slots, width), jnp.bfloat16),
            pltpu.SemaphoreType.DMA((chunks,)),
            pltpu.SemaphoreType.DMA((chunks,)),
        ],
        compiler_params=params(ALONE),
        name="relayout",
    )(expert_out)


def pick_kernel(first, hot, gate, returned, residual, shared, before, *refs):
    hidden = refs[0]
    out, base, extra, done, arrive, leave = refs[-6:]
    chunks, block, width = base.shape
    cols = slice(first, first + width)

    def loads(i):
        rows = pl.ds(i * block, block)
        return [
            pltpu.make_async_copy(residual.at[rows, cols], base.at[i], arrive.at[0, i]),
            pltpu.make_async_copy(shared.at[rows, cols], extra.at[i], arrive.at[1, i]),
        ]

    def stores(i):
        rows = pl.ds(i * block, block)
        copies = [pltpu.make_async_copy(done.at[i], out.at[rows], leave.at[0, i])]
        if first > 0:
            copies.append(pltpu.make_async_copy(done.at[i], hidden.at[rows, cols], leave.at[1, i]))
            copies.append(pltpu.make_async_copy(before.at[rows], hidden.at[rows, :first], leave.at[2, i]))
        return copies

    for i in range(chunks):
        for copy in loads(i):
            copy.start()
    for i in range(chunks):
        rows = slice(i * block, (i + 1) * block)
        picked = jnp.dot(hot[rows], returned[:, cols], preferred_element_type=jnp.float32)
        for copy in loads(i):
            copy.wait()
        total = base[i].astype(jnp.float32) + extra[i].astype(jnp.float32)
        done[i] = (total + gate[rows] * picked).astype(jnp.bfloat16)
        for copy in stores(i):
            copy.start()
    for i in range(chunks):
        for copy in stores(i):
            copy.wait()


def pick(part, hot, gate, returned, residual, shared, before):
    rows, width = residual.shape
    width = width // 2
    chunks = 2
    tile = pltpu.VMEM((chunks, rows // chunks, width), jnp.bfloat16)
    residual, shared = (pltpu.with_memory_space_constraint(a, pltpu.HBM) for a in (residual, shared))
    return pl.pallas_call(
        functools.partial(pick_kernel, part * width),
        in_specs=[vmem()] * 3 + [hbm()] * 2 + [anywhere()],
        out_specs=[hbm()] * (part + 1),
        out_shape=[
            jax.ShapeDtypeStruct((rows, columns), jnp.bfloat16)
            for columns in ((2 * width, width) if part else (width,))
        ],
        scratch_shapes=[
            tile,
            tile,
            tile,
            pltpu.SemaphoreType.DMA((2, chunks)),
            pltpu.SemaphoreType.DMA((3, chunks)),
        ],
        compiler_params=params(10),
        cost_estimate=takes(2.5),
        name="pick",
    )(hot, gate, returned, residual, shared, before)


KV_TILES, Q_TILES = 4, 2 * GROUP


def turn(x, cos, sin):
    return x * cos + pltpu.roll(x, HD // 2, 1) * sin


def gained(h, gain):
    return (h.astype(jnp.float32) * gain.astype(jnp.float32)).astype(jnp.bfloat16)


def squared(h):
    wide = h.astype(jnp.float32)
    return jnp.sum(wide * wide, axis=1, keepdims=True)


def product(x, weights, part):
    rows = pl.ds(pl.multiple_of(part * x.shape[1], x.shape[1]), x.shape[1])
    return [jnp.dot(x, w[rows, :], preferred_element_type=jnp.float32) for w in weights]


def own_kernel(where, ha, hb, gain, wk, wv, wq, part, squares):
    squares[...] = squared(ha[...]) + squared(hb[...])
    tp = where[0]
    x = jnp.concatenate([gained(ha[...], gain[2 * tp]), gained(hb[...], gain[2 * tp + 1])], axis=1)
    start = 0
    for values in product(x, (wk, wv, wq), tp):
        part[:, start : start + values.shape[1]] = values
        start += values.shape[1]


def more_kernel(where, h, gain, wk, wv, wq, old, old_squares, part, squares):
    squares[...] = old_squares[...] + squared(h[...])
    start = 0
    part_in = 2 - 2 * where[0]
    for values in product(gained(h[...], gain[part_in]), (wk, wv, wq), part_in):
        cols = slice(start, start + values.shape[1])
        part[:, cols] = old[:, cols] + values
        start += values.shape[1]


def last_kernel(where, h, gain, wk, wv, wq, old, old_squares, cos, sin, kv_mine, q_mine, other):
    total = old_squares[...] + squared(h[...])
    factor = lax.rsqrt(total / (4 * h.shape[1]) + NORM_EPS)
    part_in = 3 - 2 * where[0]
    keys, values, queries = product(gained(h[...], gain[part_in]), (wk, wv, wq), part_in)
    width = 2 * HD
    keys = (old[:, :width] + keys) * factor
    values = (old[:, width : 2 * width] + values) * factor
    queries = (old[:, 2 * width :] + queries) * (factor * (1.0 / HD**0.5 * math.log2(math.e)))

    def columns(array, head):
        return array[:, head * HD : (head + 1) * HD]

    def sides(array, axis):
        return jnp.split(array.astype(jnp.bfloat16), 2, axis=axis)

    groups = []
    for group in range(2):
        key = sides(turn(columns(keys, group), cos[...], sin[...]), 0)
        value = sides(columns(values, group).T, 1)
        kv = [key[0], value[0], key[1], value[1]]
        q = []
        for head in range(GROUP):
            q += sides(turn(columns(queries, group * GROUP + head), cos[...], sin[...]).T, 1)
        groups.append((kv, q))

    def write(mine, others):
        for i in range(KV_TILES):
            kv_mine[i // 2, i % 2] = mine[0][i]
            other[i] = others[0][i]
        for i in range(Q_TILES):
            q_mine[i // 2, i % 2] = mine[1][i]
            other[KV_TILES + i] = others[1][i]

    pl.when(where[1] == 0)(lambda: write(*groups))
    pl.when(where[1] == 1)(lambda: write(*groups[::-1]))


def project(kernel, where, ins, outs, time, name):
    return pl.pallas_call(
        kernel,
        in_specs=[smem()] + [vmem()] * len(ins),
        out_specs=[vmem()] * len(outs),
        out_shape=[jax.ShapeDtypeStruct(shape, dtype) for shape, dtype in outs],
        compiler_params=params(),
        cost_estimate=takes(time),
        name=name,
    )(where, *ins)


def project_own(where, ha, hb, gain, weights):
    rows, cols = ha.shape[0], sum(w.shape[1] for w in weights)
    outs = [((rows, cols), jnp.float32), ((rows, 1), jnp.float32)]
    return project(own_kernel, where, (ha, hb, gain, *weights), outs, 5, "project_own")


def project_more(where, h, gain, weights, partial):
    outs = [(array.shape, array.dtype) for array in partial]
    return project(more_kernel, where, (h, gain, *weights, *partial), outs, 2, "project_more")


def project_last(where, h, gain, weights, partial, cos, sin):
    q = (GROUP, 2, HD, HALF)
    shapes = [(2, 2, HALF, HD), q, (KV_TILES + Q_TILES, HALF, HD)]
    outs = [(shape, jnp.bfloat16) for shape in shapes]
    return project(last_kernel, where, (h, gain, *weights, *partial, cos, sin), outs, 2, "project_last")


ONES = 16


def attend_kernel(counts, diag, resume, finish, waits, *refs):
    flags, q, refs = refs[0], refs[1], refs[2:]
    kvs, refs = refs[: len(counts)], refs[len(counts) :]
    olds = refs[:3] if resume else ()
    refs = refs[len(olds) + waits :]
    parts = ()
    if finish:
        parts, refs = refs[:2], refs[2:]
    acc, den, top, klist, vlist = refs
    total = klist.shape[0]

    if resume:
        acc[...] = olds[0][...]
        den[...] = olds[1][...]
        top[...] = olds[2][...]
    else:
        acc[...] = jnp.zeros_like(acc)
        den[...] = jnp.zeros_like(den)
        top[...] = jnp.full_like(top, NEG_FILL)

    vlist[:, HD:, :] = jnp.ones((total, ONES, 2 * HALF), jnp.bfloat16)

    def put(place, kv, block, side):
        for core in range(2):
            span = slice(core * HALF, (core + 1) * HALF)
            klist[place, span, :] = kv[block, core, side, 0]
            vlist[place, :HD, span] = kv[block, core, side, 1]

    last = total - 2 if diag else total - 1
    front, back = jnp.int32(0), jnp.int32(last)
    start = 0
    for kv, count in zip(kvs, counts):
        for block in range(count):
            put(front, kv, block, 0)
            front = front + 1
            if diag and start + block == 0:
                continue
            early = flags[start + block]
            put(jnp.where(early == 1, back, front), kv, block, 1 - early)
            front = front + 1 - early
            back = back - early
        start += count
    n_late = front
    n_early = last - back

    def update(side, places, mask):
        keys = jnp.concatenate([klist[p] for p in places], axis=0)
        scores = []
        for head in range(GROUP):
            columns = jnp.concatenate([q[0, head, side], q[1, head, side]], axis=1)
            scores.append(jnp.dot(keys, columns, preferred_element_type=jnp.float32))
        values = jnp.concatenate([vlist[p] for p in places], axis=1)
        for head in range(GROUP):
            s = scores[head]
            if mask is not None:
                s = jnp.where(mask, s, NEG_FILL)
            old = top[side, head]
            new = jnp.maximum(old, jnp.max(s, axis=0, keepdims=True))
            weights = jnp.exp2(s - new[:1]).astype(jnp.bfloat16)
            prod = jnp.dot(values, weights, preferred_element_type=jnp.float32)
            keep = jnp.exp2(old - new)
            acc[side, head] = acc[side, head] * keep[:1] + prod[:HD]
            den[side, head] = den[side, head] * keep + prod[HD : HD + 8]
            top[side, head] = new

    if diag:
        core = flags[0]
        row = lax.broadcasted_iota(jnp.int32, (2 * HALF, 2 * HALF), 0)
        col = lax.broadcasted_iota(jnp.int32, (2 * HALF, 2 * HALF), 1)

        def own(side, carry):
            first = jnp.where(side == 0, core, 1 - core)
            key_pos = jnp.where(row < HALF, row + first * HALF, row - first * HALF)
            query_pos = jnp.where(col < HALF, col + first * HALF, col - first * HALF)
            put(total - 1, kvs[0], 0, side)
            update(side, (total - 1,), key_pos <= query_pos)
            return carry

        lax.fori_loop(0, 2, own, 0)

    quads, early_quads = n_late // 4, n_early // 4

    def four(i, carry):
        late = i < quads
        j = i - quads
        places = tuple(jnp.where(late, 4 * i + t, last - 4 * j - t) for t in range(4))
        update(jnp.where(late, 1, 0), places, None)
        return carry

    lax.fori_loop(0, quads + early_quads, four, 0)
    pairs, early_pairs = n_late // 2, n_early // 2
    rest = pairs - 2 * quads

    def two(i, carry):
        late = i < rest
        places = tuple(jnp.where(late, 4 * quads + t, last - 4 * early_quads - t) for t in range(2))
        update(jnp.where(late, 1, 0), places, None)
        return carry

    lax.fori_loop(0, rest + early_pairs - 2 * early_quads, two, 0)
    odd_late = n_late - 2 * pairs
    odd_early = n_early - 2 * early_pairs

    def one(i, carry):
        late = i < odd_late
        update(jnp.where(late, 1, 0), (jnp.where(late, n_late - 1, last - n_early + 1),), None)
        return carry

    lax.fori_loop(0, odd_late + odd_early, one, 0)

    if finish:
        write_parts(acc, den, top, parts)


def side_of(part, side):
    return part[side] if isinstance(part, tuple) else part.at[side]


def write_parts(acc, den, top, parts):
    for side in range(2):
        targets = [side_of(part, side) for part in parts]
        highs, lows = [], []
        for head in range(GROUP):
            denominator = den[side, head]
            some = denominator > 0.0
            safe = jnp.where(some, denominator, 1.0)
            inverse = jnp.where(some, 1.0 / safe, 0.0)
            value = (acc[side, head] * inverse[:1]).astype(jnp.bfloat16)
            level = jnp.where(some, top[side, head] + jnp.log2(safe), NEG_FILL)[:1]
            high = level.astype(jnp.bfloat16).astype(jnp.float32)
            highs.append(high)
            lows.append(level - high)
            for core, target in enumerate(targets):
                target[head * HD : (head + 1) * HD] = value[:, core * HALF : (core + 1) * HALF]
        filler = jnp.zeros((LOGS - 2 * GROUP, 2 * HALF), jnp.float32)
        levels = jnp.concatenate(highs + lows + [filler], axis=0).astype(jnp.bfloat16)
        for core, target in enumerate(targets):
            target[GROUP * HD :] = levels[:, core * HALF : (core + 1) * HALF]


ACC = (2, GROUP, HD, 2 * HALF)
ROWS = (2, GROUP, 8, 2 * HALF)
LOGS = 16
PART = (2, GROUP * HD + LOGS, HALF)


def attend(flags, q, kvs, state, diag=False, finish=False, after=(), time=None):
    counts = tuple(kv.shape[0] for kv in kvs)
    n = sum(counts)
    total = 2 * n
    olds = [] if state is None else list(state)
    states = (ACC, ROWS, ROWS)
    scratch = [
        pltpu.VMEM((total, 2 * HALF, HD), jnp.bfloat16),
        pltpu.VMEM((total, HD + ONES, 2 * HALF), jnp.bfloat16),
    ]
    if finish:
        shapes = [jax.ShapeDtypeStruct(PART, jnp.bfloat16)] * 2
        scratch = [pltpu.VMEM(shape, jnp.float32) for shape in states] + scratch
    else:
        shapes = [jax.ShapeDtypeStruct(shape, jnp.float32) for shape in states]
    return pl.pallas_call(
        functools.partial(attend_kernel, counts, diag, state is not None, finish, len(after)),
        in_specs=[smem()] + [vmem()] * (1 + len(kvs) + len(olds)) + [anywhere()] * len(after),
        out_specs=[vmem()] * len(shapes),
        out_shape=shapes,
        scratch_shapes=scratch,
        compiler_params=params(),
        cost_estimate=takes(1.15 * n if time is None else time),
        name="attend",
    )(flags, q, *kvs, *olds, *after)


def divide_kernel(acc, den, top, after, same, other_early, other_late):
    write_parts(acc, den, top, (same, (other_early, other_late)))


def divide(state, after):
    shapes = (PART, PART[1:], PART[1:])
    return pl.pallas_call(
        divide_kernel,
        in_specs=[vmem()] * 3 + [anywhere()],
        out_specs=[vmem()] * 3,
        out_shape=[jax.ShapeDtypeStruct(shape, jnp.bfloat16) for shape in shapes],
        compiler_params=params(),
        cost_estimate=takes(0.7),
        name="divide",
    )(*state, after)


def join_kernel(*refs):
    out = refs[-1]
    for i in range(out.shape[0]):
        out[i] = refs[i][0]


def join(blocks, after):
    return pl.pallas_call(
        join_kernel,
        in_specs=[vmem()] * len(blocks) + [anywhere()],
        out_specs=vmem(),
        out_shape=jax.ShapeDtypeStruct((len(blocks),) + blocks[0].shape[1:], jnp.bfloat16),
        compiler_params=params(),
        cost_estimate=takes(0.3),
        name="join",
    )(*blocks, after)


def merge_kernel(core, own, own_pair, sibling_early, sibling_late, sibling_pair, out):
    def read(part, side):
        terms = side_of(part, side)[GROUP * HD :].astype(jnp.float32)
        values = side_of(part, side)[: GROUP * HD].astype(jnp.float32)
        return terms[:GROUP] + terms[GROUP : 2 * GROUP], values

    sibling = (sibling_early, sibling_late)
    for group, (one, two) in ((core[0], (own, own_pair)), (1 - core[0], (sibling, sibling_pair))):
        for side in range(2):
            mine, value = read(one, side)
            other, other_value = read(two, side)
            high = jnp.maximum(mine, other)
            first = jnp.exp2(mine - high)
            second = jnp.exp2(other - high)
            weight = 1.0 / (first + second)
            first, second = first * weight, second * weight
            for head in range(GROUP):
                rows = slice(head * HD, (head + 1) * HD)
                mixed = value[rows] * first[head : head + 1] + other_value[rows] * second[head : head + 1]
                cols = pl.ds(pl.multiple_of((group * GROUP + head) * HD, HD), HD)
                out[side * HALF : (side + 1) * HALF, cols] = mixed.T.astype(jnp.bfloat16)


def merge(core, own, own_pair, sibling_early, sibling_late, sibling_pair):
    return pl.pallas_call(
        merge_kernel,
        in_specs=[smem()] + [vmem()] * 5,
        out_specs=vmem(),
        out_shape=jax.ShapeDtypeStruct((2 * HALF, 2 * GROUP * HD), jnp.bfloat16),
        compiler_params=params(),
        name="merge",
    )(core, own, own_pair, sibling_early, sibling_late, sibling_pair)


def cut_kernel(ahead, behind, after, first, second):
    half = first.shape[0]
    first[...] = ahead[:half]
    second[...] = behind[half:]


def cut(ahead, behind, after):
    shape = (ahead.shape[0] // 2,) + ahead.shape[1:]
    return pl.pallas_call(
        cut_kernel,
        in_specs=[vmem()] * 2 + [anywhere()],
        out_specs=[vmem()] * 2,
        out_shape=[jax.ShapeDtypeStruct(shape, ahead.dtype)] * 2,
        compiler_params=params(8),
        cost_estimate=takes(0.3),
        name="cut",
    )(ahead, behind, after)


def rotations(ctx_index, rows):
    row = jnp.arange(rows, dtype=jnp.int32)
    half = rows // 2
    count = NY * NZ * NX * NK
    pos = jnp.where(row < half, ctx_index * half + row, (2 * count - 1 - ctx_index) * half + row - half)
    frequency = ROPE_BASE ** (-(jnp.arange(HD // 2, dtype=jnp.float32) * 2.0 / HD))
    angles = pos.astype(jnp.float32)[:, None] * frequency[None, :]
    cos, sin = jnp.cos(angles), jnp.sin(angles)
    return jnp.concatenate([cos, cos], axis=1), jnp.concatenate([-sin, sin], axis=1)


def chip_order(y, z, x):
    return (y * NZ + z) * NX + x


def shards(residual, shared_out, expert_out, routing, gate_score, norm_gain, w_query, w_key, w_value):
    rows, half_width = residual.shape
    ctx_index = lax.axis_index("ctx")
    tp_index = lax.axis_index("tp")
    y, z, x, k = split_index(ctx_index)
    cos, sin = rotations(ctx_index, rows)

    own_experts, sources, slots, _ = expert_out.shape
    returned = lax.all_to_all(relayout(expert_out), "ctx", split_axis=0, concat_axis=0, tiled=True)
    returned = returned.reshape(sources * own_experts * slots, half_width)
    hot = choose(routing, returned.shape[0])
    (ha,) = pick(0, hot, gate_score, returned, residual, shared_out, hot)
    hidden, hb = pick(1, hot, gate_score, returned, residual, shared_out, ha)

    other_a, other_b = (lax.ppermute(h, "tp", [(0, 1), (1, 0)]) for h in (ha, hb))
    where = jnp.stack([tp_index, k])
    gain = norm_gain.reshape(4, 1, half_width // 2)
    weights = (w_key, w_value, w_query)
    partial = project_own(where, ha, hb, gain, weights)
    partial = project_more(where, other_a, gain, weights, partial)
    kv_mine, q_mine, to_other = project_last(where, other_b, gain, weights, partial, cos, sin)

    from_other = core_swap(to_other)
    block = jnp.stack([kv_mine, from_other[:KV_TILES].reshape(kv_mine.shape)])[None]
    q_own = jnp.stack([q_mine, from_other[KV_TILES:].reshape(q_mine.shape)])
    q_pair = to_pair(q_own)

    near = [first_axis(block, step) for step in (1, -1, 2)]
    own_state = attend(k.reshape(1), q_own, [block], None, diag=True, time=30)
    line = join([block] + near, own_state[2])
    steps = jnp.array([0, 1, -1, 2], jnp.int32)

    def before(first, second, chip):
        by = jnp.where(k == 0, second, first)
        bx = jnp.where(k == 0, first, second)
        return (chip_order((y + by) % NY, z, (x + bx) % NX) < chip).astype(jnp.int32)

    zero = jnp.zeros((4,), jnp.int32)
    own_flags, pair_flags = (
        jnp.concatenate([before(steps, zero + step, chip_order(y, at, x)) for step in (0, 1, -1, 2)])
        for at in (z, 1 - z)
    )
    ahead, behind = second_axis(line, 1), second_axis(line, -1)
    own_state = attend(own_flags[1:4], q_own, near, own_state, after=(line,))
    pair_state = attend(pair_flags[:4], q_pair, [line], None, after=(own_state[2],), time=7)
    far_ahead, far_behind = cut(ahead, behind, pair_state[2])
    farther = [second_axis(far_ahead, 1), second_axis(far_behind, -1)]
    pair_state = attend(pair_flags[4:12], q_pair, [ahead, behind], pair_state, after=(far_ahead,))
    pair_same, pair_other = attend(pair_flags[12:], q_pair, farther, pair_state, finish=True)
    own_pair, sibling_pair = to_pair(pair_same), to_pair_other(pair_other)
    own_state = attend(own_flags[4:], q_own, [ahead, behind] + farther, own_state, after=(pair_same,))
    own_same, *own_other = divide(own_state, sibling_pair)
    siblings = [core_swap(part) for part in own_other]
    attended = merge(k.reshape(1), own_same, own_pair, *siblings, sibling_pair)
    return hidden, attended


def solution(mesh):
    return jax.shard_map(
        shards,
        mesh=mesh,
        in_specs=(
            P("ctx", "tp"),
            P("ctx", "tp"),
            P("ctx", None, None, "tp"),
            P("ctx", None),
            P("ctx", None),
            P(),
            P(None, "tp"),
            P(None, "tp"),
            P(None, "tp"),
        ),
        out_specs=(P("ctx", "tp"), P("ctx", "tp")),
        check_vma=False,
    )
```
